32 devices in a mesh: req: 16 (over z, y, x), tensor: 2 (over core).
Axes of the slice: x: 2, y: 2, z: 4, core: 2. Of those that a mesh axis runs over, the one named last changes fastest.
Arguments:
- pre_tokens: bfloat16 [4096, 1024], P('req', 'tensor'), may hold values from -24 to 24
- dec_tokens: bfloat16 [16, 1024], P('req', 'tensor'), may hold values from -24 to 24
- req_of: int32 [16], replicated, may hold values from 0 to 15, each once
- page_table: int32 [16, 16], replicated, may hold values from -1 to 143, as said below
- page_place: int32 [144], replicated, may hold values from 0 to 143, as said below
- cache_lengths: int32 [16], replicated, may hold values from 1 to 2048, as said below
- cache_keys: bfloat16 [144, 128, 1024], P('req', None, 'tensor'), may hold values from -24 to 24
- cache_values: bfloat16 [144, 128, 1024], P('req', None, 'tensor'), may hold values from -6 to 6
- w_qkv: bfloat16 [1024, 3, 1024], P(None, None, 'tensor'), may hold values from -0.1875 to 0.1875
- w_out: bfloat16 [1024, 1024], P('tensor'), may hold values from -0.1875 to 0.1875
- ln1_gain: float32 [1024], replicated, may hold values from 0.5 to 1.5
- ln1_bias: float32 [1024], replicated, may hold values from -1 to 1
- w_up: bfloat16 [1024, 4096], P(None, 'tensor'), may hold values from -0.1875 to 0.1875
- w_down: bfloat16 [4096, 1024], P('tensor'), may hold values from -0.09375 to 0.09375
- ln2_gain: float32 [1024], replicated, may hold values from 0.5 to 1.5
- ln2_bias: float32 [1024], replicated, may hold values from -1 to 1
Outputs:
- pre_out: bfloat16 [4096, 1024], P('req', 'tensor')
- dec_out: bfloat16 [16, 1024], P('req', 'tensor')
The draws below stay inside these ranges and needn't reach their ends.
Inputs may be any that keep to these rules, and one draw needn't show every extreme that they name: `page_table`: entry j of row r is a page id for j < ceil(cache_lengths[r] / 128) and -1 after; no page id appears twice; the requests hold 136 pages together. `page_place`: a permutation; page p sits on index page_place[p] // 9 of req; one index of req holds at most 1 pages of one request, and some holds exactly 1. `cache_lengths`: some request has exactly 2048 tokens.
All inputs are finite; a program needn't handle non-finite values.
Results may differ from the reference program's by a relative error of at most 0.023.
Values may be sent and summed in bfloat16 or wider, within the bound.
No kernel may reach another device: no remote copies, remote signals or barrier semaphores. Data moves between devices by JAX's collectives and lax.ppermute only.
A program may use at most 64 MiB of HBM per device.

```python
import math
import jax
import jax.numpy as jnp
from jax import lax

D = 1024
HEADS = 16
HD = 64
FF = 4096
PAGE = 128
MAXP = 16
PRE_LEN = 256
NDEC = 16
PAGES_DEV = 9
PAGES = 144
PRE_ROWS = 4096
N_TENSOR = 2


def token_values(key, count):
    base = jnp.clip(jax.random.normal(key, (count, D), jnp.float32), -4.0, 4.0)
    return base.astype(jnp.bfloat16)


def draw_pre_tokens(key, part):
    return token_values(key, PRE_ROWS)


def draw_dec_tokens(key, part):
    return token_values(jax.random.fold_in(key, 7), NDEC)


def draw_cache_keys(key, part):
    base = 2.0 * jnp.clip(jax.random.normal(key, (PAGES, PAGE, D), jnp.float32), -4.0, 4.0)
    return base.astype(jnp.bfloat16)


def page_layout(key):
    pair_order = jax.random.permutation(jax.random.fold_in(key, 101), NDEC).astype(jnp.int32)
    firsts = jax.random.randint(jax.random.fold_in(key, 102), (NDEC // 2,), 1, MAXP + 1).astype(jnp.int32)
    firsts = firsts.at[0].set(MAXP)
    counts = jnp.zeros((NDEC,), jnp.int32).at[pair_order[0::2]].set(firsts).at[pair_order[1::2]].set(MAXP + 1 - firsts)
    alloc_order = jax.random.permutation(jax.random.fold_in(key, 103), NDEC).astype(jnp.int32)
    ordered = counts[alloc_order]
    begin_ordered = jnp.cumsum(ordered) - ordered
    begin = jnp.zeros((NDEC,), jnp.int32).at[alloc_order].set(begin_ordered.astype(jnp.int32))
    labels = jax.random.permutation(jax.random.fold_in(key, 104), PAGES).astype(jnp.int32)
    steps = jnp.arange(MAXP, dtype=jnp.int32)
    positions = begin[:, None] + steps[None, :]
    valid = steps[None, :] < counts[:, None]
    table = jnp.where(valid, labels[jnp.clip(positions, 0, PAGES - 1)], -1).astype(jnp.int32)
    inverse = jnp.zeros((PAGES,), jnp.int32).at[labels].set(jnp.arange(PAGES, dtype=jnp.int32))
    place = (inverse % NDEC * PAGES_DEV + inverse // NDEC).astype(jnp.int32)
    tails = jax.random.randint(jax.random.fold_in(key, 105), (NDEC,), 1, PAGE + 1).astype(jnp.int32)
    lengths = (counts - 1) * PAGE + tails
    lengths = lengths.at[pair_order[0]].set(MAXP * PAGE).astype(jnp.int32)
    return (table, place, lengths)


def draw_page_table(key, part):
    return page_layout(key)[0]


def draw_page_place(key, part):
    return page_layout(key)[1]


def draw_cache_lengths(key, part):
    return page_layout(key)[2]


def block_levels(stream_key, extent, shards, low, top_value):
    level, own = 1.0, jax.random.fold_in(stream_key, 6)
    for axis_at, parts in shards:
        heights = jnp.exp(jax.random.uniform(jax.random.fold_in(own, axis_at), (parts,), jnp.float32, low / len(shards), top_value / len(shards)))
        level = level * jnp.repeat(heights, extent[axis_at] // parts).reshape([-1 if axis == axis_at else 1 for axis in range(len(extent))])
    return level


def scatter_about(stream_key, extent, scale, limit, split=(), held_as=jnp.bfloat16):
    entries = scale * jax.random.normal(stream_key, extent, jnp.float32)
    if split:
        entries = entries * block_levels(stream_key, extent, split, -0.22, 0.18)
    return jnp.clip(entries, -limit, limit).astype(held_as)


def setup_inputs(seed: int = 0) -> dict:
    streams_of = jax.random.split(jax.random.key(seed), 17)
    pre_tokens = draw_pre_tokens(jax.random.fold_in(streams_of[16], 71), 0)
    dec_tokens = draw_dec_tokens(jax.random.fold_in(streams_of[16], 71), 0)
    req_of = jax.random.permutation(streams_of[2], NDEC).astype(jnp.int32)
    page_table = draw_page_table(jax.random.fold_in(streams_of[16], 71), 0)
    page_place = draw_page_place(jax.random.fold_in(streams_of[16], 71), 0)
    cache_lengths = draw_cache_lengths(jax.random.fold_in(streams_of[16], 71), 0)
    cache_keys = draw_cache_keys(jax.random.fold_in(streams_of[16], 71), 0)
    cache_values = scatter_about(streams_of[7], (PAGES, PAGE, D), 1.0, 6.0, ((0, 16), (2, 2)))
    w_qkv = scatter_about(streams_of[8], (D, 3, D), D ** -0.5, 0.1875, ((2, 2),))
    w_out = scatter_about(streams_of[9], (D, D), D ** -0.5, 0.1875, ((0, 2),))
    ln1_gain = jnp.clip(1.0 + 0.1 * jax.random.normal(streams_of[10], (D,), jnp.float32), 0.5, 1.5)
    ln1_bias = scatter_about(streams_of[11], (D,), 0.2, 1.0, (), jnp.float32)
    w_up = scatter_about(streams_of[12], (D, FF), D ** -0.5, 0.1875, ((1, 2),))
    w_down = scatter_about(streams_of[13], (FF, D), FF ** -0.5, 0.09375, ((0, 2),))
    ln2_gain = jnp.clip(1.0 + 0.1 * jax.random.normal(streams_of[14], (D,), jnp.float32), 0.5, 1.5)
    ln2_bias = scatter_about(streams_of[15], (D,), 0.2, 1.0, (), jnp.float32)
    return dict(pre_tokens=pre_tokens, dec_tokens=dec_tokens, req_of=req_of, page_table=page_table, page_place=page_place, cache_lengths=cache_lengths, cache_keys=cache_keys, cache_values=cache_values, w_qkv=w_qkv, w_out=w_out, ln1_gain=ln1_gain, ln1_bias=ln1_bias, w_up=w_up, w_down=w_down, ln2_gain=ln2_gain, ln2_bias=ln2_bias)


norm_eps = 1e-05
neg_large = -1e+30

def norm_rows(total, gain, shift):
    mean = lax.optimization_barrier(jnp.mean(total, axis=-1, keepdims=True))
    centered = total - mean
    var = lax.optimization_barrier(jnp.mean(centered * centered, axis=-1, keepdims=True))
    return centered * lax.rsqrt(var + norm_eps) * gain + shift

def rounded(values):
    return lax.optimization_barrier(values.astype(jnp.bfloat16)).astype(jnp.float32)

def group_sum(left, right, group_width):
    total = jnp.zeros((left.shape[0], right.shape[1]), jnp.float32)
    for group in range(N_TENSOR):
        low = group * group_width
        term = jnp.dot(left[:, low:low + group_width], right[low:low + group_width], preferred_element_type=jnp.float32)
        total = total + rounded(term)
    return total

def reference(pre_tokens, dec_tokens, req_of, page_table, page_place, cache_lengths, cache_keys, cache_values, w_qkv, w_out, ln1_gain, ln1_bias, w_up, w_down, ln2_gain, ln2_bias):
    scale = 1.0 / math.sqrt(HD)
    flat_qkv = w_qkv.reshape(D, 3 * D)

    def one_slot(inputs):
        pre_rows, dec_row, request = inputs
        rows = jnp.concatenate([pre_rows, dec_row[None]], axis=0)
        mixed = rounded(jnp.dot(rows, flat_qkv, preferred_element_type=jnp.float32))
        mixed = mixed.reshape(PRE_LEN + 1, 3, HEADS, HD)
        query = mixed[:, 0]
        keyed = mixed[:, 1]
        valued = mixed[:, 2]
        scores = jnp.einsum('qhd,khd->hqk', query[:PRE_LEN], keyed[:PRE_LEN]) * scale
        row_pos = jnp.arange(PRE_LEN, dtype=jnp.int32)
        causal = row_pos[:, None] >= row_pos[None, :]
        scores = jnp.where(causal[None], scores, neg_large)
        top = lax.optimization_barrier(jnp.max(scores, axis=-1, keepdims=True))
        weights = jnp.where(causal[None], jnp.exp(scores - top), 0.0)
        total = lax.optimization_barrier(jnp.sum(weights, axis=-1))
        pre_context = jnp.einsum('hqk,khd->qhd', rounded(weights), valued[:PRE_LEN]) / jnp.transpose(total)[:, :, None]
        pre_context = pre_context.astype(jnp.bfloat16).reshape(PRE_LEN, D)
        slots = page_place[jnp.maximum(page_table[request], 0)]
        keys = cache_keys[slots].reshape(MAXP * PAGE, HEADS, HD).astype(jnp.float32)
        values = cache_values[slots].reshape(MAXP * PAGE, HEADS, HD).astype(jnp.float32)
        keys = jnp.concatenate([keys, keyed[PRE_LEN][None]], axis=0)
        values = jnp.concatenate([values, valued[PRE_LEN][None]], axis=0)
        positions = jnp.arange(MAXP * PAGE, dtype=jnp.int32)
        usable = jnp.concatenate([positions < cache_lengths[request], jnp.ones((1,), dtype=bool)])
        dec_scores = jnp.einsum('hd,khd->hk', query[PRE_LEN], keys) * scale
        dec_scores = jnp.where(usable[None], dec_scores, neg_large)
        dec_top = lax.optimization_barrier(jnp.max(dec_scores, axis=-1, keepdims=True))
        dec_weights = jnp.where(usable[None], jnp.exp(dec_scores - dec_top), 0.0)
        dec_total = lax.optimization_barrier(jnp.sum(dec_weights, axis=-1))
        dec_context = jnp.einsum('hk,khd->hd', rounded(dec_weights), values) / dec_total[:, None]
        dec_context = dec_context.astype(jnp.bfloat16).reshape(1, D)
        context = jnp.concatenate([pre_context, dec_context], axis=0)
        attn = group_sum(context, w_out, D // N_TENSOR)
        first = norm_rows(rows.astype(jnp.float32) + attn, ln1_gain, ln1_bias).astype(jnp.bfloat16)
        hidden = jax.nn.gelu(jnp.dot(first, w_up, preferred_element_type=jnp.float32), approximate=False).astype(jnp.bfloat16)
        mlp = group_sum(hidden, w_down, FF // N_TENSOR)
        first_wide = lax.optimization_barrier(first).astype(jnp.float32)
        result = norm_rows(first_wide + mlp, ln2_gain, ln2_bias).astype(jnp.bfloat16)
        return (result[:PRE_LEN], result[PRE_LEN])
    pre_out, dec_out = lax.map(one_slot, (pre_tokens.reshape(NDEC, PRE_LEN, D), dec_tokens, req_of))
    return (pre_out.reshape(PRE_ROWS, D), dec_out)
```

```python
import functools
import math

import jax
import jax.numpy as jnp
from jax import lax
from jax.experimental import pallas as pl
from jax.experimental.pallas import tpu as pltpu
from jax.sharding import PartitionSpec as P

HD = 64
LANES = 128
NORM_EPS = 1e-05
NEG_LARGE = -1e30
BF16 = jnp.bfloat16
F32 = jnp.float32

VMEM = pl.BlockSpec(memory_space=pltpu.VMEM)
SMEM = pl.BlockSpec(memory_space=pltpu.SMEM)


def params(mib):
    return pltpu.CompilerParams(vmem_limit_bytes=mib << 20)


def cost(flops, nbytes, trans=0):
    return pl.CostEstimate(flops=flops, bytes_accessed=nbytes, transcendentals=trans)


def dot(left, right):
    return jnp.dot(left, right, preferred_element_type=F32)


def dot_t(left, right):
    return lax.dot_general(left, right, (((1,), (1,)), ((), ())), preferred_element_type=F32)


def norm_rows(total, gain, shift):
    mean = jnp.mean(total, axis=-1, keepdims=True)
    centered = total - mean
    var = jnp.mean(centered * centered, axis=-1, keepdims=True)
    return centered * lax.rsqrt(var + NORM_EPS) * gain + shift


def gelu(x):
    return 0.5 * x * (1.0 + lax.erf(x * (1.0 / math.sqrt(2.0))))


def head_mask(rows, cols):
    head = lax.broadcasted_iota(jnp.int32, (rows, cols), 0)
    lane = lax.broadcasted_iota(jnp.int32, (rows, cols), 1)
    return lane // HD == head


def find_pages(me, pages_here, page_len, req_of, table, place, lengths, info, entry, slot_of):
    n_req, max_pages = table.shape
    for p in range(pages_here + 1):
        entry[p] = -1

    def one_slot(i, carry):
        slot_of[req_of[i]] = i
        return carry

    lax.fori_loop(0, n_req, one_slot, 0)

    def one_request(r, carry):
        for j in range(max_pages):
            page = table[r, j]
            local = place[jnp.maximum(page, 0)] - me * pages_here
            here = (page >= 0) & (local >= 0) & (local < pages_here)
            entry[jnp.where(here, local, pages_here)] = r * max_pages + j
        return carry

    lax.fori_loop(0, n_req, one_request, 0)
    for p in range(pages_here):
        at = entry[p]
        known = at >= 0
        at = jnp.maximum(at, 0)
        r = lax.div(at, max_pages)
        j = at - r * max_pages
        info[p] = jnp.where(known, slot_of[r], -1)
        info[pages_here + p] = jnp.minimum(lengths[r] - j * page_len, page_len)


def prefill_kernel(
    n_chunks, pages_here, page_len, place_ref, req_of, table, place, lengths, *refs
):
    chunks = refs[:n_chunks]
    w_qkv, w_out, full, term, info, entry, slot_of, ctx = refs[n_chunks:]
    me = place_ref[0]
    find_pages(me, pages_here, page_len, req_of, table, place, lengths, info, entry, slot_of)
    pre_len = full.shape[0]
    cols = w_qkv.shape[2]
    parts = [0.0, 0.0, 0.0]
    for c, chunk in enumerate(chunks):
        wide = chunk.shape[1]
        off = pl.multiple_of(place_ref[1 + c], LANES)
        x = chunk[...]
        full[:, pl.ds(off, wide)] = x
        for s in range(3):
            parts[s] = parts[s] + dot(x, w_qkv[s, pl.ds(off, wide), :])
    q, k, v = (part.astype(BF16) for part in parts)
    q = q * jnp.asarray(1.0 / math.sqrt(HD), BF16)
    lane = lax.broadcasted_iota(jnp.int32, (pre_len, LANES), 1)
    low = lane < HD
    row = lax.broadcasted_iota(jnp.int32, (2 * pre_len, pre_len), 0)
    col = lax.broadcasted_iota(jnp.int32, (2 * pre_len, pre_len), 1)
    causal = jnp.where(row >= pre_len, row - pre_len, row) >= col
    zero = jnp.zeros((), BF16)
    for g in range(cols // LANES):
        at = slice(g * LANES, (g + 1) * LANES)
        qg = q[:, at]
        both = jnp.concatenate([jnp.where(low, qg, zero), jnp.where(low, zero, qg)], axis=0)
        scores = jnp.where(causal, dot_t(both, k[:, at]), NEG_LARGE)
        top = jnp.max(scores, axis=-1, keepdims=True)
        weights = jnp.exp(scores - top)
        total = jnp.sum(weights, axis=-1, keepdims=True)
        out = dot(weights.astype(BF16), v[:, at]) / total
        ctx[:, at] = jnp.where(low, out[:pre_len], out[pre_len:]).astype(BF16)
    term[...] = dot(ctx[...], w_out[...]).astype(BF16)


def prefill(chunks, offsets, me, req_of, table, place, lengths, w_qkv, w_out, pages_here, page_len):
    pre_len = chunks[0].shape[0]
    width, cols = w_qkv.shape[1:]
    n_req = table.shape[0]
    where = jnp.stack([me, *offsets]).astype(jnp.int32)
    flops = 2 * pre_len * width * cols * 4 + 8 * pre_len * pre_len * cols
    return pl.pallas_call(
        functools.partial(prefill_kernel, len(chunks), pages_here, page_len),
        in_specs=[SMEM] * 5 + [VMEM] * (len(chunks) + 2),
        out_specs=(VMEM, VMEM, SMEM),
        out_shape=(
            jax.ShapeDtypeStruct((pre_len, width), BF16),
            jax.ShapeDtypeStruct((pre_len, width), BF16),
            jax.ShapeDtypeStruct((2 * pages_here,), jnp.int32),
        ),
        scratch_shapes=[
            pltpu.SMEM((pages_here + 1,), jnp.int32),
            pltpu.SMEM((n_req,), jnp.int32),
            pltpu.VMEM((pre_len, cols), BF16),
        ],
        compiler_params=params(24),
        cost_estimate=cost(flops, 2 * width * cols * 4 + 8 * pre_len * width, cols * pre_len),
        name="prefill",
    )(where, req_of, table, place, lengths, *chunks, w_qkv, w_out)


def pages_kernel(n_tensor, me_ref, info, tokens, w_qkv, keys, values, sent, own, row, q_scr, x_scr):
    n_req, twice, _ = sent.shape
    width, cols = w_qkv.shape[1:]
    pieces = cols // LANES
    pages_here, page_len = keys.shape[:2]
    heads = max(8, cols // HD)
    me = me_ref[0]
    x = jnp.concatenate(
        [tokens[t * n_req : (t + 1) * n_req, r, :] for t in range(n_tensor) for r in range(pieces)],
        axis=1,
    )
    x_scr[...] = x
    row[...] = x_scr[pl.ds(me, 1), :]
    x = x.astype(BF16)
    q_scr[0] = dot(x, w_qkv[0]).astype(BF16).astype(F32) * (1.0 / math.sqrt(HD))
    q_scr[1] = dot(x, w_qkv[1]).astype(BF16).astype(F32)
    q_scr[2] = dot(x, w_qkv[2]).astype(BF16).astype(F32)
    mask = head_mask(heads, cols)
    token = lax.broadcasted_iota(jnp.int32, (heads, page_len), 1)

    def spread(per_head):
        return jnp.sum(jnp.where(mask, per_head, 0.0), axis=0, keepdims=True)

    def put(ref, at, context, level):
        for r in range(pieces):
            ref[at, r : r + 1, :] = context[:, r * LANES : (r + 1) * LANES]
            ref[at, pieces + r : pieces + r + 1, :] = level[:, r * LANES : (r + 1) * LANES]

    half = lax.broadcasted_iota(jnp.int32, sent.shape, 1)
    sent[...] = jnp.where(half < pieces, 0.0, NEG_LARGE)
    mine = pl.ds(me, 1)
    own_q, own_k, own_v = (q_scr[s, mine, :] for s in range(3))
    own_score = jnp.sum(jnp.where(mask, own_q * own_k, 0.0), axis=1, keepdims=True)
    put(own, 0, own_v, spread(own_score))
    for p in range(pages_here):
        slot = info[p]
        usable = info[pages_here + p]
        query = q_scr[0, pl.ds(jnp.maximum(slot, 0), 1), :]
        query = jnp.where(mask, query, 0.0).astype(BF16)
        scores = jnp.where(token < usable, dot_t(query, keys[p]), NEG_LARGE)
        top = jnp.max(scores, axis=-1, keepdims=True)
        weights = jnp.exp(scores - top)
        total = jnp.sum(weights, axis=-1, keepdims=True)
        summed = dot(weights.astype(BF16), values[p]) / total

        @pl.when(slot >= 0)
        def _():
            put(sent, slot, spread(summed), spread(top + jnp.log(total)))


def pages(me, info, tokens, w_qkv, keys, values, n_req, n_tensor):
    width, cols = w_qkv.shape[1:]
    pages_here, page_len = keys.shape[:2]
    twice = 2 * (cols // LANES)
    return pl.pallas_call(
        functools.partial(pages_kernel, n_tensor),
        in_specs=[SMEM] * 2 + [VMEM] * 4,
        out_specs=(VMEM, VMEM, VMEM),
        out_shape=(
            jax.ShapeDtypeStruct((n_req, twice, LANES), F32),
            jax.ShapeDtypeStruct((1, twice, LANES), F32),
            jax.ShapeDtypeStruct((1, width), F32),
        ),
        scratch_shapes=[pltpu.VMEM((3, n_req, cols), F32), pltpu.VMEM((n_req, width), F32)],
        compiler_params=params(16),
        cost_estimate=cost(2 * 16 * width * cols * 3, 2 * width * cols * 3 + 4 * pages_here * page_len * cols),
        name="pages",
    )(jnp.reshape(me, (1,)), info, tokens, w_qkv, keys, values)


def join_kernel(got, own, w_out, term):
    pieces = got.shape[1] // 2
    total = 0.0
    for r in range(pieces):
        level = got[:, pieces + r, :]
        own_level = own[0, pieces + r : pieces + r + 1, :]
        top = jnp.maximum(jnp.max(level, axis=0, keepdims=True), own_level)
        share = jnp.exp(level - top)
        own_share = jnp.exp(own_level - top)
        numer = jnp.sum(share * got[:, r, :], axis=0, keepdims=True) + own_share * own[0, r : r + 1, :]
        denom = jnp.sum(share, axis=0, keepdims=True) + own_share
        context = (numer / denom).astype(BF16)
        total = total + dot(context, w_out[r * LANES : (r + 1) * LANES, :])
    term[...] = total.astype(BF16).astype(F32)


def join(got, own, w_out):
    cols, width = w_out.shape
    return pl.pallas_call(
        join_kernel,
        in_specs=[VMEM] * 3,
        out_specs=VMEM,
        out_shape=jax.ShapeDtypeStruct((1, width), F32),
        compiler_params=params(8),
        cost_estimate=cost(16 * cols * width, 2 * cols * width),
        name="join",
    )(got, own, w_out)


def mlp_kernel(n_terms, tile, rows, *refs):
    terms = refs[:n_terms]
    gain, shift, w_up, w_down, first_ref, term = refs[n_terms:]
    attn = terms[0][...].astype(F32)
    for other in terms[1:]:
        attn = attn + other[...].astype(F32)
    first = norm_rows(rows[...].astype(F32) + attn, gain[...], shift[...]).astype(BF16)
    first_ref[...] = first.astype(first_ref.dtype)
    total = 0.0
    for at in range(0, w_up.shape[1], tile):
        hidden = gelu(dot(first, w_up[:, at : at + tile])).astype(BF16)
        total = total + dot(hidden, w_down[at : at + tile, :])
    term[...] = total.astype(BF16).astype(term.dtype)


def mlp(rows, terms, gain, shift, w_up, w_down, name):
    count, width = rows.shape
    units = w_up.shape[1]
    dtype = rows.dtype
    return pl.pallas_call(
        functools.partial(mlp_kernel, len(terms), min(512, units)),
        in_specs=[VMEM] * (5 + len(terms)),
        out_specs=(VMEM, VMEM),
        out_shape=(
            jax.ShapeDtypeStruct((count, width), dtype),
            jax.ShapeDtypeStruct((count, width), dtype),
        ),
        compiler_params=params(28),
        cost_estimate=cost(4 * count * width * units, 4 * width * units, count * units),
        name=name,
    )(rows, *terms, gain, shift, w_up, w_down)


def finish_kernel(n_terms, part_ref, first, *refs):
    terms = refs[:n_terms]
    gain, shift, out, scr = refs[n_terms:]
    total = first[...].astype(F32)
    mlp_sum = terms[0][...].astype(F32)
    for other in terms[1:]:
        mlp_sum = mlp_sum + other[...].astype(F32)
    total = total + mlp_sum
    mean = jnp.mean(total, axis=-1, keepdims=True)
    scr[...] = total - mean
    var = jnp.mean(scr[...] * scr[...], axis=-1, keepdims=True)
    cols = out.shape[1]
    at = pl.ds(pl.multiple_of(part_ref[0] * cols, LANES), cols)
    out[...] = (scr[:, at] * lax.rsqrt(var + NORM_EPS) * gain[:, at] + shift[:, at]).astype(BF16)


def finish(part, first, terms, gain, shift, cols, name):
    count, width = first.shape
    return pl.pallas_call(
        functools.partial(finish_kernel, len(terms)),
        in_specs=[SMEM] + [VMEM] * (3 + len(terms)),
        out_specs=VMEM,
        out_shape=jax.ShapeDtypeStruct((count, cols), BF16),
        scratch_shapes=[pltpu.VMEM((count, width), F32)],
        compiler_params=params(12),
        cost_estimate=cost(20 * count * width, 8 * count * width),
        name=name,
    )(jnp.reshape(part, (1,)), first, *terms, gain, shift)


def local(
    pre_tokens,
    dec_tokens,
    req_of,
    page_table,
    page_place,
    cache_lengths,
    cache_keys,
    cache_values,
    w_qkv,
    w_out,
    ln1_gain,
    ln1_bias,
    w_up,
    w_down,
    ln2_gain,
    ln2_bias,
):
    cols = w_qkv.shape[2]
    n_req = lax.axis_size("req")
    n_tensor = lax.axis_size("tensor")
    me = lax.axis_index("req").astype(jnp.int32)
    part = lax.axis_index("tensor").astype(jnp.int32)
    pages_here, page_len = cache_keys.shape[:2]
    w_qkv = jnp.transpose(w_qkv, (1, 0, 2))
    gain1, bias1, gain2, bias2 = (
        jnp.reshape(v, (1, -1)) for v in (ln1_gain, ln1_bias, ln2_gain, ln2_bias)
    )

    def swapped(x):
        return lax.ppermute(x, "tensor", [(0, 1), (1, 0)])

    def gathered_terms(x):
        if n_tensor == 2:
            return (x, swapped(x))
        return (lax.psum(x, "tensor"),)

    spread = jnp.broadcast_to(
        dec_tokens.astype(F32).reshape(1, cols // LANES, LANES),
        (n_tensor * n_req, cols // LANES, LANES),
    )
    tokens = lax.all_to_all(spread, ("tensor", "req"), split_axis=0, concat_axis=0, tiled=True)
    if n_tensor == 2:
        chunks = (pre_tokens, swapped(pre_tokens))
        offsets = (part * cols, (1 - part) * cols)
    else:
        chunks = (lax.all_gather(pre_tokens, "tensor", axis=1, tiled=True),)
        offsets = (jnp.zeros((), jnp.int32),)
    rows, attn_term, info = prefill(
        chunks, offsets, me, req_of, page_table, page_place, cache_lengths, w_qkv, w_out, pages_here, page_len
    )
    attn_terms = gathered_terms(attn_term)
    sent, own, dec_row = pages(me, info, tokens, w_qkv, cache_keys, cache_values, n_req, n_tensor)
    got = lax.all_to_all(sent, "req", split_axis=0, concat_axis=0, tiled=True)
    first, mlp_term = mlp(rows, attn_terms, gain1, bias1, w_up, w_down, "pre_mlp")
    pre_out = finish(part, first, gathered_terms(mlp_term), gain2, bias2, cols, "pre_norm")
    dec_terms = gathered_terms(join(got, own, w_out))
    dec_first, dec_mlp = mlp(dec_row, dec_terms, gain1, bias1, w_up, w_down, "dec_mlp")
    dec_out = finish(part, dec_first, gathered_terms(dec_mlp), gain2, bias2, cols, "dec_norm")
    return (pre_out, dec_out)


def solution(mesh):
    in_specs = (
        P("req", "tensor"),
        P("req", "tensor"),
        P(),
        P(),
        P(),
        P(),
        P("req", None, "tensor"),
        P("req", None, "tensor"),
        P(None, None, "tensor"),
        P("tensor", None),
        P(),
        P(),
        P(None, "tensor"),
        P("tensor", None),
        P(),
        P(),
    )
    out_specs = (P("req", "tensor"), P("req", "tensor"))
    return jax.shard_map(local, mesh=mesh, in_specs=in_specs, out_specs=out_specs, check_vma=False)
```

```python
import functools
import math

import jax
import jax.numpy as jnp
from jax import lax
from jax.experimental import pallas as pl
from jax.experimental.pallas import tpu as pltpu
from jax.sharding import PartitionSpec as P

HD = 64
LANES = 128
TAIL = 16
NORM_EPS = 1e-05
NEG_LARGE = -1e30
BF16 = jnp.bfloat16
F32 = jnp.float32

VMEM = pl.BlockSpec(memory_space=pltpu.VMEM)
SMEM = pl.BlockSpec(memory_space=pltpu.SMEM)
HBM = pl.BlockSpec(memory_space=pltpu.HBM)


def in_hbm(x):
    return pltpu.with_memory_space_constraint(x, pltpu.HBM)


def like(x):
    return jax.ShapeDtypeStruct(x.shape, x.dtype)


def params(mib):
    return pltpu.CompilerParams(vmem_limit_bytes=mib << 20)


def cost(flops=1):
    return pl.CostEstimate(flops=flops, bytes_accessed=1, transcendentals=0)


def dot(left, right):
    return jnp.dot(left, right, preferred_element_type=F32)


def dot_t(left, right):
    return lax.dot_general(left, right, (((1,), (1,)), ((), ())), preferred_element_type=F32)


def norm_rows(total, gain, shift):
    mean = jnp.mean(total, axis=-1, keepdims=True)
    centered = total - mean
    var = jnp.mean(centered * centered, axis=-1, keepdims=True)
    return centered * lax.rsqrt(var + NORM_EPS) * gain + shift


def gelu(x):
    return 0.5 * x * (1.0 + lax.erf(x * (1.0 / math.sqrt(2.0))))


def head_mask(rows, cols):
    head = lax.broadcasted_iota(jnp.int32, (rows, cols), 0)
    lane = lax.broadcasted_iota(jnp.int32, (rows, cols), 1)
    return lane // HD == head


def find_pages(me, pages_here, page_len, req_of, table, place, lengths, info, entry, slot_of):
    n_req, max_pages = table.shape
    for p in range(pages_here + 1):
        entry[p] = -1

    def one_slot(i, carry):
        slot_of[req_of[i]] = i
        return carry

    lax.fori_loop(0, n_req, one_slot, 0)

    def one_request(r, carry):
        for j in range(max_pages):
            page = table[r, j]
            local = place[jnp.maximum(page, 0)] - me * pages_here
            here = (page >= 0) & (local >= 0) & (local < pages_here)
            entry[jnp.where(here, local, pages_here)] = r * max_pages + j
        return carry

    lax.fori_loop(0, n_req, one_request, 0)
    for p in range(pages_here):
        at = entry[p]
        known = at >= 0
        at = jnp.maximum(at, 0)
        r = lax.div(at, max_pages)
        j = at - r * max_pages
        info[p] = jnp.where(known, slot_of[r], -1)
        info[pages_here + p] = jnp.minimum(lengths[r] - j * page_len, page_len)


def start_kernel(
    where, token, req_of_hbm, table_hbm, place_hbm, lengths_hbm, w_qkv_hbm, out, info, w_q, *refs
):
    req_of, table, place, lengths, entry, slot_of, sems = refs
    weights = pltpu.make_async_copy(w_qkv_hbm.at[0], w_q, sems.at[4])
    copies = [
        pltpu.make_async_copy(source, target, sems.at[i])
        for i, (source, target) in enumerate(
            ((req_of_hbm, req_of), (table_hbm, table), (place_hbm, place), (lengths_hbm, lengths))
        )
    ]
    for copy in (*copies, weights):
        copy.start()
    for r in range(out.shape[1]):
        piece = token[:, r * LANES : (r + 1) * LANES].astype(F32)
        out[:, r, :] = jnp.broadcast_to(piece, (out.shape[0], LANES))
    for copy in copies:
        copy.wait()
    find_pages(where[0], info.shape[0] // 2, where[1], req_of, table, place, lengths, info, entry, slot_of)
    weights.wait()


def start(where, token, lists, w_qkv, count, pages_here):
    pieces = token.shape[1] // LANES
    return pl.pallas_call(
        start_kernel,
        in_specs=[SMEM, VMEM] + [HBM] * 5,
        out_specs=[VMEM, SMEM, VMEM],
        out_shape=[
            jax.ShapeDtypeStruct((count, pieces, LANES), F32),
            jax.ShapeDtypeStruct((2 * pages_here,), jnp.int32),
            jax.ShapeDtypeStruct(w_qkv.shape[1:], BF16),
        ],
        scratch_shapes=[pltpu.SMEM(x.shape, jnp.int32) for x in lists]
        + [
            pltpu.SMEM((pages_here + 1,), jnp.int32),
            pltpu.SMEM(lists[0].shape, jnp.int32),
            pltpu.SemaphoreType.DMA((5,)),
        ],
        compiler_params=params(8),
        cost_estimate=cost(),
        name="start",
    )(where, token, *(in_hbm(x) for x in (*lists, w_qkv)))


def pages_kernel(n_tensor, n_chunks, where, info, *refs):
    chunks = refs[:n_chunks]
    tokens, w_q, keys, values, sent, rows, q_scr, x_scr, sent_scr, sems = refs[n_chunks:]
    n_req = sent.shape[0]
    cols = w_q.shape[1]
    pieces = cols // LANES
    pages_here, page_len = keys.shape[:2]
    heads = max(8, cols // HD)
    pre_len = chunks[0].shape[0]
    copies = []
    for c, chunk in enumerate(chunks):
        band = pl.ds(pl.multiple_of(where[2 + c], LANES), chunk.shape[1])
        copies.append(pltpu.make_async_copy(chunk, rows.at[pl.ds(0, pre_len), band], sems.at[c]))
        copies[-1].start()
    me = where[0]
    x = jnp.concatenate(
        [tokens[t * n_req : (t + 1) * n_req, r, :] for t in range(n_tensor) for r in range(pieces)],
        axis=1,
    )
    x_scr[...] = x
    q_scr[...] = dot(x.astype(BF16), w_q[...]).astype(BF16).astype(F32) * (1.0 / math.sqrt(HD))
    tail = rows.shape[0] - pre_len
    first = lax.broadcasted_iota(jnp.int32, (tail, rows.shape[1]), 0) == 0
    rows[pre_len:, :] = jnp.where(first, x_scr[pl.ds(me, 1), :], 0.0).astype(BF16)
    mask = head_mask(heads, cols)
    token = lax.broadcasted_iota(jnp.int32, (heads, page_len), 1)

    def spread(per_head):
        return jnp.sum(jnp.where(mask, per_head, 0.0), axis=0, keepdims=True)

    half = lax.broadcasted_iota(jnp.int32, sent_scr.shape, 1)
    sent_scr[...] = jnp.where(half < pieces, 0.0, NEG_LARGE)
    scores = []
    for p in range(pages_here):
        query = q_scr[pl.ds(jnp.maximum(info[p], 0), 1), :]
        query = jnp.where(mask, query, 0.0).astype(BF16)
        scores.append(jnp.where(token < info[pages_here + p], dot_t(query, keys[p]), NEG_LARGE))
    scores = jnp.concatenate(scores, axis=0)
    top = jnp.max(scores, axis=-1, keepdims=True)
    weights = jnp.exp(scores - top)
    total = jnp.sum(weights, axis=-1, keepdims=True)
    level = top + jnp.log(total)
    weights = weights.astype(BF16)
    for p in range(pages_here):
        at = slice(p * heads, (p + 1) * heads)
        context = spread(dot(weights[at], values[p]) / total[at])
        lse = spread(level[at])
        slot = info[p]
        slot = jnp.where(slot < 0, n_req, slot)
        for r in range(pieces):
            sent_scr[slot, r : r + 1, :] = context[:, r * LANES : (r + 1) * LANES]
            sent_scr[slot, pieces + r : pieces + r + 1, :] = lse[:, r * LANES : (r + 1) * LANES]
    sent[...] = sent_scr[:n_req]
    for copy in copies:
        copy.wait()


def pages(where, info, chunks, tokens, w_q, keys, values, n_req, n_tensor):
    width, cols = w_q.shape
    twice = 2 * (cols // LANES)
    return pl.pallas_call(
        functools.partial(pages_kernel, n_tensor, len(chunks)),
        in_specs=[SMEM] * 2 + [HBM] * len(chunks) + [VMEM] * 4,
        out_specs=[VMEM] * 2,
        out_shape=[
            jax.ShapeDtypeStruct((n_req, twice, LANES), F32),
            jax.ShapeDtypeStruct((chunks[0].shape[0] + TAIL, width), BF16),
        ],
        scratch_shapes=[
            pltpu.VMEM((n_req, cols), F32),
            pltpu.VMEM((n_req, width), F32),
            pltpu.VMEM((n_req + 1, twice, LANES), F32),
            pltpu.SemaphoreType.DMA((len(chunks),)),
        ],
        compiler_params=params(12),
        cost_estimate=cost(),
        name="pages",
    )(where, info, *(in_hbm(x) for x in chunks), tokens, w_q, keys, values)


def attend_kernel(w_qkv_hbm, w_out_hbm, rows, w_q, got, term, w_kv, w_out, ctx, sems):
    copies = [
        pltpu.make_async_copy(w_qkv_hbm.at[1], w_kv.at[0], sems.at[0]),
        pltpu.make_async_copy(w_qkv_hbm.at[2], w_kv.at[1], sems.at[1]),
        pltpu.make_async_copy(w_out_hbm, w_out, sems.at[2]),
    ]
    for copy in copies:
        copy.start()
    count = rows.shape[0]
    pre_len = count - TAIL
    cols = w_q.shape[1]
    pieces = cols // LANES
    x = rows[...]
    q = dot(x, w_q[...]).astype(BF16) * jnp.asarray(1.0 / math.sqrt(HD), BF16)
    copies[0].wait()
    k = dot(x, w_kv[0]).astype(BF16)
    copies[1].wait()
    v = dot(x, w_kv[1]).astype(BF16)

    heads = max(8, cols // HD)
    mask = head_mask(heads, cols)
    own_q, own_k, own_v = (part[pre_len:].astype(F32)[:1] for part in (q, k, v))
    own_score = jnp.sum(jnp.where(mask, own_q * own_k, 0.0), axis=1, keepdims=True)
    own_level = jnp.sum(jnp.where(mask, own_score, 0.0), axis=0, keepdims=True)
    is_first = lax.broadcasted_iota(jnp.int32, (TAIL, LANES), 0) == 0

    half = pre_len // 2
    low = lax.broadcasted_iota(jnp.int32, (half, LANES), 1) < HD
    row = lax.broadcasted_iota(jnp.int32, (2 * half, half), 0)
    col = lax.broadcasted_iota(jnp.int32, (2 * half, half), 1)
    causal = jnp.where(row >= half, row - half, row) >= col
    zero = jnp.zeros((), BF16)
    ones = jnp.ones((pre_len, LANES), BF16)
    for g in range(pieces):
        at = slice(g * LANES, (g + 1) * LANES)
        kg = k[:pre_len, at]
        vg = jnp.concatenate([v[:pre_len, at], ones], axis=1)
        for block in range(2):
            mine = slice(block * half, (block + 1) * half)
            qg = q[mine, at]
            both = jnp.concatenate([jnp.where(low, qg, zero), jnp.where(low, zero, qg)], axis=0)
            scores = jnp.where(causal, dot_t(both, kg[mine]), NEG_LARGE)
            if block:
                scores = jnp.concatenate([dot_t(both, kg[:half]), scores], axis=1)
            top = jnp.max(scores, axis=-1, keepdims=True)
            weights = jnp.exp(scores - top).astype(BF16)
            out = dot(weights, vg[: (block + 1) * half])
            out = out[:, :LANES] / out[:, LANES:]
            ctx[mine, at] = jnp.where(low, out[:half], out[half:]).astype(BF16)

        level = got[:, pieces + g, :]
        top = jnp.maximum(jnp.max(level, axis=0, keepdims=True), own_level[:, at])
        share = jnp.exp(level - top)
        own_share = jnp.exp(own_level[:, at] - top)
        numer = jnp.sum(share * got[:, g, :], axis=0, keepdims=True) + own_share * own_v[:, at]
        denom = jnp.sum(share, axis=0, keepdims=True) + own_share
        ctx[pre_len:, at] = jnp.where(is_first, numer / denom, 0.0).astype(BF16)
    copies[2].wait()
    term[...] = dot(ctx[...], w_out[...]).astype(BF16)


def attend(rows, w_q, got, w_qkv, w_out):
    width, cols = w_q.shape
    return pl.pallas_call(
        attend_kernel,
        in_specs=[HBM] * 2 + [VMEM] * 3,
        out_specs=VMEM,
        out_shape=like(rows),
        scratch_shapes=[
            pltpu.VMEM((2, width, cols), BF16),
            pltpu.VMEM((cols, width), BF16),
            pltpu.VMEM((rows.shape[0], cols), BF16),
            pltpu.SemaphoreType.DMA((3,)),
        ],
        compiler_params=params(20),
        cost_estimate=cost(6_000_000_000),
        name="attend",
    )(in_hbm(w_qkv), in_hbm(w_out), rows, w_q, got)


def mlp_kernel(n_terms, tile, rows, *refs):
    terms = refs[:n_terms]
    gain, shift, w_up, w_down, first_ref, term = refs[n_terms:]
    attn = terms[0][...].astype(F32)
    for other in terms[1:]:
        attn = attn + other[...].astype(F32)
    first = norm_rows(rows[...].astype(F32) + attn, gain[...], shift[...]).astype(BF16)
    first_ref[...] = first
    total = 0.0
    for at in range(0, w_up.shape[1], tile):
        hidden = gelu(dot(first, w_up[:, at : at + tile])).astype(BF16)
        total = total + dot(hidden, w_down[at : at + tile, :])
    term[...] = total.astype(BF16)


def mlp(rows, terms, gain, shift, w_up, w_down):
    units = w_up.shape[1]
    return pl.pallas_call(
        functools.partial(mlp_kernel, len(terms), min(512, units)),
        in_specs=[VMEM] * (5 + len(terms)),
        out_specs=[VMEM] * 2,
        out_shape=[like(rows), like(rows)],
        compiler_params=params(28),
        cost_estimate=cost(),
        name="mlp",
    )(rows, *terms, gain, shift, w_up, w_down)


def finish_kernel(n_terms, where, first, *refs):
    terms = refs[:n_terms]
    gain, shift, pre_out, dec_out, scr = refs[n_terms:]
    mlp_sum = terms[0][...].astype(F32)
    for other in terms[1:]:
        mlp_sum = mlp_sum + other[...].astype(F32)
    total = first[...].astype(F32) + mlp_sum
    centered = total - jnp.mean(total, axis=-1, keepdims=True)
    scr[...] = centered
    var = jnp.mean(centered * centered, axis=-1, keepdims=True)
    pre_len, cols = pre_out.shape
    at = pl.ds(pl.multiple_of(where[2], LANES), cols)
    out = (scr[:, at] * lax.rsqrt(var + NORM_EPS) * gain[:, at] + shift[:, at]).astype(BF16)
    pre_out[...] = out[:pre_len]
    dec_out[...] = out[pre_len:].astype(F32)[:1].astype(BF16)


def finish(where, first, terms, gain, shift, cols):
    count, width = first.shape
    return pl.pallas_call(
        functools.partial(finish_kernel, len(terms)),
        in_specs=[SMEM] + [VMEM] * (3 + len(terms)),
        out_specs=[VMEM] * 2,
        out_shape=[
            jax.ShapeDtypeStruct((count - TAIL, cols), BF16),
            jax.ShapeDtypeStruct((1, cols), BF16),
        ],
        scratch_shapes=[pltpu.VMEM((count, width), F32)],
        compiler_params=params(12),
        cost_estimate=cost(),
        name="finish",
    )(where, first, *terms, gain, shift)


def local(
    pre_tokens,
    dec_tokens,
    req_of,
    page_table,
    page_place,
    cache_lengths,
    cache_keys,
    cache_values,
    w_qkv,
    w_out,
    ln1_gain,
    ln1_bias,
    w_up,
    w_down,
    ln2_gain,
    ln2_bias,
):
    cols = w_qkv.shape[2]
    n_req = lax.axis_size("req")
    n_tensor = lax.axis_size("tensor")
    me = lax.axis_index("req").astype(jnp.int32)
    part = lax.axis_index("tensor").astype(jnp.int32)
    pages_here, page_len = cache_keys.shape[:2]
    w_qkv = jnp.transpose(w_qkv, (1, 0, 2))
    gain1, bias1, gain2, bias2 = (
        jnp.reshape(v, (1, -1)) for v in (ln1_gain, ln1_bias, ln2_gain, ln2_bias)
    )

    def swapped(x):
        return lax.ppermute(x, "tensor", [(0, 1), (1, 0)])

    def gathered_terms(x):
        if n_tensor == 2:
            return (x, swapped(x))
        return (lax.psum(x, "tensor"),)

    if n_tensor == 2:
        chunks = (pre_tokens, swapped(pre_tokens))
        offsets = (part * cols, (1 - part) * cols)
    else:
        chunks = (lax.all_gather(pre_tokens, "tensor", axis=1, tiled=True),)
        offsets = (jnp.zeros((), jnp.int32),)
    where = jnp.stack([me, jnp.full((), page_len, jnp.int32), *offsets])
    mine = jnp.stack([me, jnp.zeros((), jnp.int32), part * cols])
    lists = (req_of, page_table, page_place, cache_lengths)
    spread, info, w_q = start(where, dec_tokens, lists, w_qkv, n_tensor * n_req, pages_here)
    tokens = lax.all_to_all(spread, ("tensor", "req"), split_axis=0, concat_axis=0, tiled=True)
    sent, rows = pages(where, info, chunks, tokens, w_q, cache_keys, cache_values, n_req, n_tensor)
    got = lax.all_to_all(sent, "req", split_axis=0, concat_axis=0, tiled=True)
    attn_term = attend(rows, w_q, got, w_qkv, w_out)
    first, mlp_term = mlp(rows, gathered_terms(attn_term), gain1, bias1, w_up, w_down)
    return tuple(finish(mine, first, gathered_terms(mlp_term), gain2, bias2, cols))


def solution(mesh):
    in_specs = (
        P("req", "tensor"),
        P("req", "tensor"),
        P(),
        P(),
        P(),
        P(),
        P("req", None, "tensor"),
        P("req", None, "tensor"),
        P(None, None, "tensor"),
        P("tensor", None),
        P(),
        P(),
        P(None, "tensor"),
        P("tensor", None),
        P(),
        P(),
    )
    out_specs = (P("req", "tensor"), P("req", "tensor"))
    return jax.shard_map(local, mesh=mesh, in_specs=in_specs, out_specs=out_specs, check_vma=False)
```

```python
import functools
import math

import jax
import jax.numpy as jnp
from jax import lax
from jax.experimental import pallas as pl
from jax.experimental.pallas import tpu as pltpu
from jax.sharding import PartitionSpec as P

HD = 64
LANES = 128
TAIL = 16
NORM_EPS = 1e-05
NEG_LARGE = -1e30
BF16 = jnp.bfloat16
F32 = jnp.float32

VMEM = pl.BlockSpec(memory_space=pltpu.VMEM)
HBM = pl.BlockSpec(memory_space=pltpu.HBM)


def in_hbm(x):
    return pltpu.with_memory_space_constraint(x, pltpu.HBM)


def like(x):
    return jax.ShapeDtypeStruct(x.shape, x.dtype)


def params(mib):
    return pltpu.CompilerParams(vmem_limit_bytes=mib << 20)


def cost(flops=1):
    return pl.CostEstimate(flops=flops, bytes_accessed=1, transcendentals=0)


def dot(left, right):
    return jnp.dot(left, right, preferred_element_type=F32)


def dot_t(left, right):
    return lax.dot_general(left, right, (((1,), (1,)), ((), ())), preferred_element_type=F32)


def norm_rows(total, gain, shift):
    mean = jnp.mean(total, axis=-1, keepdims=True)
    centered = total - mean
    var = jnp.mean(centered * centered, axis=-1, keepdims=True)
    return centered * lax.rsqrt(var + NORM_EPS) * gain + shift


def gelu(x):
    return 0.5 * x * (1.0 + lax.erf(x * (1.0 / math.sqrt(2.0))))


def head_mask(rows, cols):
    head = lax.broadcasted_iota(jnp.int32, (rows, cols), 0)
    lane = lax.broadcasted_iota(jnp.int32, (rows, cols), 1)
    return lane // HD == head


def start_kernel(token_hbm, w_qkv_hbm, out, w_q, token, sems):
    weights = pltpu.make_async_copy(w_qkv_hbm.at[0], w_q, sems.at[0])
    fetch = pltpu.make_async_copy(token_hbm, token, sems.at[1])
    fetch.start()
    weights.start()
    fetch.wait()
    for r in range(out.shape[1]):
        piece = token[:, r * LANES : (r + 1) * LANES].astype(F32)
        out[:, r, :] = jnp.broadcast_to(piece, (out.shape[0], LANES))
    weights.wait()


def start(token, w_qkv, count):
    pieces = token.shape[1] // LANES
    return pl.pallas_call(
        start_kernel,
        in_specs=[HBM] * 2,
        out_specs=[VMEM] * 2,
        out_shape=[
            jax.ShapeDtypeStruct((count, pieces, LANES), F32),
            jax.ShapeDtypeStruct(w_qkv.shape[1:], BF16),
        ],
        scratch_shapes=[pltpu.VMEM(token.shape, BF16), pltpu.SemaphoreType.DMA((2,))],
        compiler_params=params(8),
        cost_estimate=cost(),
        name="start",
    )(in_hbm(token), in_hbm(w_qkv))


def pages_kernel(
    n_tensor,
    n_chunks,
    own_chunk,
    req_of,
    table,
    place,
    lengths,
    tokens,
    w_q,
    keys,
    values,
    *refs,
):
    others = refs[: n_chunks - 1]
    sent, rows, x_scr, sem = refs[n_chunks - 1 :]
    n_req, max_pages = table.shape
    cols = w_q.shape[1]
    pieces = cols // LANES
    pages_here, page_len = keys.shape[:2]
    heads = max(8, cols // HD)
    pre_len, wide = own_chunk.shape
    me = lax.axis_index("req")
    part = lax.axis_index("tensor")
    offset = part * wide if n_chunks > 1 else 0
    band = pl.ds(pl.multiple_of(offset, LANES), wide) if n_chunks > 1 else slice(None)
    copy = pltpu.make_async_copy(own_chunk, rows.at[pl.ds(0, pre_len), band], sem)
    copy.start()
    x = jnp.concatenate(
        [tokens[t * n_req : (t + 1) * n_req, r, :] for t in range(n_tensor) for r in range(pieces)],
        axis=1,
    )
    x_scr[...] = x
    q = dot(x.astype(BF16), w_q[...]).astype(BF16).astype(F32) * (1.0 / math.sqrt(HD))

    slot_row = lax.broadcasted_iota(jnp.int32, (n_req, n_req), 0)
    slot_col = lax.broadcasted_iota(jnp.int32, (n_req, n_req), 1)
    request = jnp.sum(jnp.where(slot_row == slot_col, req_of[...], 0), axis=1, keepdims=True)
    served = request == slot_col
    length = jnp.sum(jnp.where(served, lengths[...], 0), axis=1, keepdims=True)
    ids = jnp.dot(
        served.astype(F32),
        table[...].astype(F32),
        precision=lax.Precision.HIGHEST,
        preferred_element_type=F32,
    ).astype(jnp.int32)
    at_page = lax.broadcasted_iota(jnp.int32, (n_req, max_pages), 1)
    left = length - at_page * page_len
    page_ids = lax.broadcasted_iota(jnp.int32, place.shape, 1)
    owners = []
    usable = []
    for p in range(pages_here):
        page = jnp.sum(jnp.where(place[...] == me * pages_here + p, page_ids, 0), axis=1, keepdims=True)
        hit = ids == page
        owners.append(jnp.sum(jnp.where(hit, 1.0, 0.0), axis=1, keepdims=True))
        count = jnp.sum(jnp.where(hit, left, 0), axis=1, keepdims=True)
        usable.append(jnp.sum(count, axis=0, keepdims=True))

    mask = head_mask(heads, cols)
    token = lax.broadcasted_iota(jnp.int32, (heads, page_len), 1)

    def spread(per_head):
        return jnp.sum(jnp.where(mask, per_head, 0.0), axis=0, keepdims=True)

    scores = []
    for p in range(pages_here):
        query = jnp.sum(owners[p] * q, axis=0, keepdims=True)
        query = jnp.where(mask, query, 0.0).astype(BF16)
        scores.append(jnp.where(token < usable[p], dot_t(query, keys[p]), NEG_LARGE))
    scores = jnp.concatenate(scores, axis=0)
    top = jnp.max(scores, axis=-1, keepdims=True)
    weights = jnp.exp(scores - top)
    total = jnp.sum(weights, axis=-1, keepdims=True)
    level = top + jnp.log(total)
    weights = weights.astype(BF16)
    context = jnp.zeros((n_req, cols), F32)
    levels = (1.0 - sum(owners)) * jnp.full((n_req, cols), NEG_LARGE, F32)
    for p in range(pages_here):
        at = slice(p * heads, (p + 1) * heads)
        context = context + owners[p] * spread(dot(weights[at], values[p]) / total[at])
        levels = levels + owners[p] * spread(level[at])
    for r in range(pieces):
        sent[:, r, :] = context[:, r * LANES : (r + 1) * LANES]
        sent[:, pieces + r, :] = levels[:, r * LANES : (r + 1) * LANES]

    tail = rows.shape[0] - pre_len
    first = lax.broadcasted_iota(jnp.int32, (tail, rows.shape[1]), 0) == 0
    rows[pre_len:, :] = jnp.where(first, x_scr[pl.ds(me, 1), :], 0.0).astype(BF16)
    for other in others:
        rows[:pre_len, pl.ds(pl.multiple_of((1 - part) * wide, LANES), wide)] = other[...]
    copy.wait()


def pages(chunks, lists, tokens, w_q, keys, values, n_tensor):
    width, cols = w_q.shape
    n_req = lists[0].shape[0]
    twice = 2 * (cols // LANES)
    req_of, table, place, lengths = lists
    lists = (req_of.reshape(1, -1), table, place.reshape(1, -1), lengths.reshape(1, -1))
    return pl.pallas_call(
        functools.partial(pages_kernel, n_tensor, len(chunks)),
        in_specs=[HBM] + [VMEM] * (7 + len(chunks)),
        out_specs=[VMEM] * 2,
        out_shape=[
            jax.ShapeDtypeStruct((n_req, twice, LANES), F32),
            jax.ShapeDtypeStruct((chunks[0].shape[0] + TAIL, width), BF16),
        ],
        scratch_shapes=[pltpu.VMEM((n_req, width), F32), pltpu.SemaphoreType.DMA],
        compiler_params=params(12),
        cost_estimate=cost(),
        name="pages",
    )(in_hbm(chunks[0]), *lists, tokens, w_q, keys, values, *chunks[1:])


def attend_kernel(w_qkv_hbm, w_out_hbm, rows, w_q, got, term, w_kv, w_out, ctx, sems):
    copies = [
        pltpu.make_async_copy(w_qkv_hbm.at[1], w_kv.at[0], sems.at[0]),
        pltpu.make_async_copy(w_qkv_hbm.at[2], w_kv.at[1], sems.at[1]),
        pltpu.make_async_copy(w_out_hbm, w_out, sems.at[2]),
    ]
    for copy in copies:
        copy.start()
    count = rows.shape[0]
    pre_len = count - TAIL
    cols = w_q.shape[1]
    pieces = cols // LANES
    x = rows[...]
    q = dot(x, w_q[...]).astype(BF16) * jnp.asarray(1.0 / math.sqrt(HD), BF16)
    copies[0].wait()
    k = dot(x, w_kv[0]).astype(BF16)
    copies[1].wait()
    v = dot(x, w_kv[1]).astype(BF16)

    heads = max(8, cols // HD)
    mask = head_mask(heads, cols)
    own_q, own_k, own_v = (part[pre_len:].astype(F32)[:1] for part in (q, k, v))
    own_score = jnp.sum(jnp.where(mask, own_q * own_k, 0.0), axis=1, keepdims=True)
    own_level = jnp.sum(jnp.where(mask, own_score, 0.0), axis=0, keepdims=True)
    is_first = lax.broadcasted_iota(jnp.int32, (TAIL, LANES), 0) == 0

    half = pre_len // 2
    low = lax.broadcasted_iota(jnp.int32, (half, LANES), 1) < HD
    row = lax.broadcasted_iota(jnp.int32, (2 * half, half), 0)
    col = lax.broadcasted_iota(jnp.int32, (2 * half, half), 1)
    causal = jnp.where(row >= half, row - half, row) >= col
    zero = jnp.zeros((), BF16)
    ones = jnp.ones((pre_len, LANES), BF16)
    for g in range(pieces):
        at = slice(g * LANES, (g + 1) * LANES)
        kg = k[:pre_len, at]
        vg = jnp.concatenate([v[:pre_len, at], ones], axis=1)
        for block in range(2):
            mine = slice(block * half, (block + 1) * half)
            qg = q[mine, at]
            both = jnp.concatenate([jnp.where(low, qg, zero), jnp.where(low, zero, qg)], axis=0)
            scores = jnp.where(causal, dot_t(both, kg[mine]), NEG_LARGE)
            if block:
                scores = jnp.concatenate([dot_t(both, kg[:half]), scores], axis=1)
            top = jnp.max(scores, axis=-1, keepdims=True)
            weights = jnp.exp(scores - top).astype(BF16)
            out = dot(weights, vg[: (block + 1) * half])
            out = out[:, :LANES] / out[:, LANES:]
            ctx[mine, at] = jnp.where(low, out[:half], out[half:]).astype(BF16)

        level = got[:, pieces + g, :]
        top = jnp.maximum(jnp.max(level, axis=0, keepdims=True), own_level[:, at])
        share = jnp.exp(level - top)
        own_share = jnp.exp(own_level[:, at] - top)
        numer = jnp.sum(share * got[:, g, :], axis=0, keepdims=True) + own_share * own_v[:, at]
        denom = jnp.sum(share, axis=0, keepdims=True) + own_share
        ctx[pre_len:, at] = jnp.where(is_first, numer / denom, 0.0).astype(BF16)
    copies[2].wait()
    term[...] = dot(ctx[...], w_out[...]).astype(BF16)


def attend(rows, w_q, got, w_qkv, w_out):
    width, cols = w_q.shape
    return pl.pallas_call(
        attend_kernel,
        in_specs=[HBM] * 2 + [VMEM] * 3,
        out_specs=VMEM,
        out_shape=like(rows),
        scratch_shapes=[
            pltpu.VMEM((2, width, cols), BF16),
            pltpu.VMEM((cols, width), BF16),
            pltpu.VMEM((rows.shape[0], cols), BF16),
            pltpu.SemaphoreType.DMA((3,)),
        ],
        compiler_params=params(20),
        cost_estimate=cost(6_000_000_000),
        name="attend",
    )(in_hbm(w_qkv), in_hbm(w_out), rows, w_q, got)


def mlp_kernel(n_terms, tile, rows, *refs):
    terms = refs[:n_terms]
    gain, shift, w_up, w_down, first_ref, term = refs[n_terms:]
    attn = terms[0][...].astype(F32)
    for other in terms[1:]:
        attn = attn + other[...].astype(F32)
    first = norm_rows(rows[...].astype(F32) + attn, gain[...], shift[...]).astype(BF16)
    first_ref[...] = first
    total = 0.0
    for at in range(0, w_up.shape[1], tile):
        hidden = gelu(dot(first, w_up[:, at : at + tile])).astype(BF16)
        total = total + dot(hidden, w_down[at : at + tile, :])
    term[...] = total.astype(BF16)


def mlp(rows, terms, gain, shift, w_up, w_down):
    units = w_up.shape[1]
    return pl.pallas_call(
        functools.partial(mlp_kernel, len(terms), min(512, units)),
        in_specs=[VMEM] * (5 + len(terms)),
        out_specs=[VMEM] * 2,
        out_shape=[like(rows), like(rows)],
        compiler_params=params(28),
        cost_estimate=cost(),
        name="mlp",
    )(rows, *terms, gain, shift, w_up, w_down)


def finish_kernel(n_terms, first, *refs):
    terms = refs[:n_terms]
    gain, shift, pre_out, dec_out, scr = refs[n_terms:]
    mlp_sum = terms[0][...].astype(F32)
    for other in terms[1:]:
        mlp_sum = mlp_sum + other[...].astype(F32)
    total = first[...].astype(F32) + mlp_sum
    centered = total - jnp.mean(total, axis=-1, keepdims=True)
    scr[...] = centered
    var = jnp.mean(centered * centered, axis=-1, keepdims=True)
    pre_len, cols = pre_out.shape
    at = pl.ds(pl.multiple_of(lax.axis_index("tensor") * cols, LANES), cols)
    out = (scr[:, at] * lax.rsqrt(var + NORM_EPS) * gain[:, at] + shift[:, at]).astype(BF16)
    pre_out[...] = out[:pre_len]
    dec_out[...] = out[pre_len:].astype(F32)[:1].astype(BF16)


def finish(first, terms, gain, shift, cols):
    count, width = first.shape
    return pl.pallas_call(
        functools.partial(finish_kernel, len(terms)),
        in_specs=[VMEM] * (3 + len(terms)),
        out_specs=[VMEM] * 2,
        out_shape=[
            jax.ShapeDtypeStruct((count - TAIL, cols), BF16),
            jax.ShapeDtypeStruct((1, cols), BF16),
        ],
        scratch_shapes=[pltpu.VMEM((count, width), F32)],
        compiler_params=params(12),
        cost_estimate=cost(),
        name="finish",
    )(first, *terms, gain, shift)


def local(
    pre_tokens,
    dec_tokens,
    req_of,
    page_table,
    page_place,
    cache_lengths,
    cache_keys,
    cache_values,
    w_qkv,
    w_out,
    ln1_gain,
    ln1_bias,
    w_up,
    w_down,
    ln2_gain,
    ln2_bias,
):
    cols = w_qkv.shape[2]
    n_req = lax.axis_size("req")
    n_tensor = lax.axis_size("tensor")
    w_qkv = jnp.transpose(w_qkv, (1, 0, 2))
    gain1, bias1, gain2, bias2 = (
        jnp.reshape(v, (1, -1)) for v in (ln1_gain, ln1_bias, ln2_gain, ln2_bias)
    )

    def swapped(x):
        return lax.ppermute(x, "tensor", [(0, 1), (1, 0)])

    def gathered_terms(x):
        if n_tensor == 2:
            return (x, swapped(x))
        return (lax.psum(x, "tensor"),)

    if n_tensor == 2:
        chunks = (pre_tokens, swapped(pre_tokens))
    else:
        chunks = (lax.all_gather(pre_tokens, "tensor", axis=1, tiled=True),)
    lists = (req_of, page_table, page_place, cache_lengths)
    spread, w_q = start(dec_tokens, w_qkv, n_tensor * n_req)
    tokens = lax.all_to_all(spread, ("tensor", "req"), split_axis=0, concat_axis=0, tiled=True)
    sent, rows = pages(chunks, lists, tokens, w_q, cache_keys, cache_values, n_tensor)
    got = lax.all_to_all(sent, "req", split_axis=0, concat_axis=0, tiled=True)
    attn_term = attend(rows, w_q, got, w_qkv, w_out)
    first, mlp_term = mlp(rows, gathered_terms(attn_term), gain1, bias1, w_up, w_down)
    return tuple(finish(first, gathered_terms(mlp_term), gain2, bias2, cols))


def solution(mesh):
    in_specs = (
        P("req", "tensor"),
        P("req", "tensor"),
        P(),
        P(),
        P(),
        P(),
        P("req", None, "tensor"),
        P("req", None, "tensor"),
        P(None, None, "tensor"),
        P("tensor", None),
        P(),
        P(),
        P(None, "tensor"),
        P("tensor", None),
        P(),
        P(),
    )
    out_specs = (P("req", "tensor"), P("req", "tensor"))
    return jax.shard_map(local, mesh=mesh, in_specs=in_specs, out_specs=out_specs, check_vma=False)
```

```python
import functools
import math

import jax
import jax.numpy as jnp
from jax import lax
from jax.experimental import pallas as pl
from jax.experimental.pallas import tpu as pltpu
from jax.sharding import PartitionSpec as P

HD = 64
LANES = 128
TAIL = 16
NORM_EPS = 1e-05
NEG_LARGE = -1e30
BF16 = jnp.bfloat16
F32 = jnp.float32

VMEM = pl.BlockSpec(memory_space=pltpu.VMEM)
HBM = pl.BlockSpec(memory_space=pltpu.HBM)


def in_hbm(x):
    return pltpu.with_memory_space_constraint(x, pltpu.HBM)


def like(x):
    return jax.ShapeDtypeStruct(x.shape, x.dtype)


def params(mib):
    return pltpu.CompilerParams(vmem_limit_bytes=mib << 20)


def cost(flops=1):
    return pl.CostEstimate(flops=flops, bytes_accessed=1, transcendentals=0)


def start_all(copies):
    @pl.loop(0, jnp.where(lax.axis_index("req") >= 0, 1, 0))
    def _(_):
        for copy in copies:
            copy.start()


def dot(left, right):
    return jnp.dot(left, right, preferred_element_type=F32)


def dot_t(left, right):
    return lax.dot_general(left, right, (((1,), (1,)), ((), ())), preferred_element_type=F32)


def norm_rows(total, gain, shift):
    mean = jnp.mean(total, axis=-1, keepdims=True)
    centered = total - mean
    var = jnp.mean(centered * centered, axis=-1, keepdims=True)
    return centered * lax.rsqrt(var + NORM_EPS) * gain + shift


def gelu(x):
    return 0.5 * x * (1.0 + lax.erf(x * (1.0 / math.sqrt(2.0))))


def head_mask(rows, cols):
    head = lax.broadcasted_iota(jnp.int32, (rows, cols), 0)
    lane = lax.broadcasted_iota(jnp.int32, (rows, cols), 1)
    return lane // HD == head


def start_kernel(token_hbm, w_qkv_hbm, out, w_q, token, sems):
    weights = pltpu.make_async_copy(w_qkv_hbm.at[0], w_q, sems.at[0])
    fetch = pltpu.make_async_copy(token_hbm, token, sems.at[1])
    start_all((fetch, weights))
    fetch.wait()
    for r in range(out.shape[1]):
        piece = token[:, r * LANES : (r + 1) * LANES].astype(F32)
        out[:, r, :] = jnp.broadcast_to(piece, (out.shape[0], LANES))
    weights.wait()


def start(token, w_qkv, count):
    pieces = token.shape[1] // LANES
    return pl.pallas_call(
        start_kernel,
        in_specs=[HBM] * 2,
        out_specs=[VMEM] * 2,
        out_shape=[
            jax.ShapeDtypeStruct((count, pieces, LANES), F32),
            jax.ShapeDtypeStruct(w_qkv.shape[1:], BF16),
        ],
        scratch_shapes=[pltpu.VMEM(token.shape, BF16), pltpu.SemaphoreType.DMA((2,))],
        compiler_params=params(8),
        cost_estimate=cost(),
        name="start",
    )(in_hbm(token), in_hbm(w_qkv))


def pages_kernel(
    n_tensor,
    n_chunks,
    own_chunk,
    w_qkv_hbm,
    req_of,
    table,
    place,
    lengths,
    tokens,
    w_q,
    keys,
    values,
    *refs,
):
    others = refs[: n_chunks - 1]
    sent, rows, w_k, x_scr, sems = refs[n_chunks - 1 :]
    n_req, max_pages = table.shape
    cols = w_q.shape[1]
    pieces = cols // LANES
    pages_here, page_len = keys.shape[:2]
    heads = max(8, cols // HD)
    pre_len, wide = own_chunk.shape
    me = lax.axis_index("req")
    part = lax.axis_index("tensor")
    copies = [pltpu.make_async_copy(w_qkv_hbm.at[1], w_k, sems.at[0])]
    for c, chunk in enumerate((own_chunk, *others)):
        offset = part * wide if c == 0 else (1 - part) * wide
        band = pl.ds(pl.multiple_of(offset, LANES), wide) if others else slice(None)
        copies.append(pltpu.make_async_copy(chunk, rows.at[pl.ds(0, pre_len), band], sems.at[1 + c]))
    start_all(copies)
    x = jnp.concatenate(
        [tokens[t * n_req : (t + 1) * n_req, r, :] for t in range(n_tensor) for r in range(pieces)],
        axis=1,
    )
    x_scr[...] = x
    q = dot(x.astype(BF16), w_q[...]).astype(BF16).astype(F32) * (1.0 / math.sqrt(HD))

    slot_row = lax.broadcasted_iota(jnp.int32, (n_req, n_req), 0)
    slot_col = lax.broadcasted_iota(jnp.int32, (n_req, n_req), 1)
    request = jnp.sum(jnp.where(slot_row == slot_col, req_of[...], 0), axis=1, keepdims=True)
    served = request == slot_col
    length = jnp.sum(jnp.where(served, lengths[...], 0), axis=1, keepdims=True)
    ids = jnp.dot(
        served.astype(F32),
        table[...].astype(F32),
        precision=lax.Precision.HIGHEST,
        preferred_element_type=F32,
    ).astype(jnp.int32)
    at_page = lax.broadcasted_iota(jnp.int32, (n_req, max_pages), 1)
    left = length - at_page * page_len
    page_ids = lax.broadcasted_iota(jnp.int32, place.shape, 1)
    owners = []
    usable = []
    for p in range(pages_here):
        page = jnp.sum(jnp.where(place[...] == me * pages_here + p, page_ids, 0), axis=1, keepdims=True)
        hit = ids == page
        owners.append(jnp.sum(jnp.where(hit, 1.0, 0.0), axis=1, keepdims=True))
        count = jnp.sum(jnp.where(hit, left, 0), axis=1, keepdims=True)
        usable.append(jnp.sum(count, axis=0, keepdims=True))

    mask = head_mask(heads, cols)
    token = lax.broadcasted_iota(jnp.int32, (heads, page_len), 1)

    def spread(per_head):
        return jnp.sum(jnp.where(mask, per_head, 0.0), axis=0, keepdims=True)

    scores = []
    for p in range(pages_here):
        query = jnp.sum(owners[p] * q, axis=0, keepdims=True)
        query = jnp.where(mask, query, 0.0).astype(BF16)
        scores.append(jnp.where(token < usable[p], dot_t(query, keys[p]), NEG_LARGE))
    scores = jnp.concatenate(scores, axis=0)
    top = jnp.max(scores, axis=-1, keepdims=True)
    weights = jnp.exp(scores - top)
    total = jnp.sum(weights, axis=-1, keepdims=True)
    level = top + jnp.log(total)
    weights = weights.astype(BF16)
    context = jnp.zeros((n_req, cols), F32)
    levels = (1.0 - sum(owners)) * jnp.full((n_req, cols), NEG_LARGE, F32)
    for p in range(pages_here):
        at = slice(p * heads, (p + 1) * heads)
        context = context + owners[p] * spread(dot(weights[at], values[p]) / total[at])
        levels = levels + owners[p] * spread(level[at])
    to = pl.ds(pl.multiple_of(part * n_req, n_req), n_req) if n_tensor == 2 else slice(None)
    if n_tensor == 2:
        sent[...] = jnp.zeros(sent.shape, F32)
    for r in range(pieces):
        sent[to, r, :] = context[:, r * LANES : (r + 1) * LANES]
        sent[to, pieces + r, :] = levels[:, r * LANES : (r + 1) * LANES]

    tail = rows.shape[0] - pre_len
    first = lax.broadcasted_iota(jnp.int32, (tail, rows.shape[1]), 0) == 0
    rows[pre_len:, :] = jnp.where(first, x_scr[pl.ds(me, 1), :], 0.0).astype(BF16)
    for copy in copies:
        copy.wait()


def pages(chunks, w_qkv, lists, tokens, w_q, keys, values, n_tensor):
    width, cols = w_q.shape
    n_req = lists[0].shape[0]
    twice = 2 * (cols // LANES)
    req_of, table, place, lengths = lists
    lists = (req_of.reshape(1, -1), table, place.reshape(1, -1), lengths.reshape(1, -1))
    return pl.pallas_call(
        functools.partial(pages_kernel, n_tensor, len(chunks)),
        in_specs=[HBM] * 2 + [VMEM] * (7 + len(chunks)),
        out_specs=[VMEM] * 3,
        out_shape=[
            jax.ShapeDtypeStruct((n_req * (2 if n_tensor == 2 else 1), twice, LANES), F32),
            jax.ShapeDtypeStruct((chunks[0].shape[0] + TAIL, width), BF16),
            like(w_q),
        ],
        scratch_shapes=[pltpu.VMEM((n_req, width), F32), pltpu.SemaphoreType.DMA((1 + len(chunks),))],
        compiler_params=params(12),
        cost_estimate=cost(),
        name="pages",
    )(in_hbm(chunks[0]), in_hbm(w_qkv), *lists, tokens, w_q, keys, values, *chunks[1:])


def attend_kernel(n_req, w_qkv_hbm, w_out_hbm, rows, w_q, w_k, got, term, w_v, w_out, ctx, sems):
    copies = [
        pltpu.make_async_copy(w_qkv_hbm.at[2], w_v, sems.at[0]),
        pltpu.make_async_copy(w_out_hbm, w_out, sems.at[1]),
    ]
    start_all(copies)
    count = rows.shape[0]
    pre_len = count - TAIL
    cols = w_q.shape[1]
    pieces = cols // LANES
    half = pre_len // 2
    x = rows[...]
    q = dot(x, w_q[...]).astype(BF16) * jnp.asarray(1.0 / math.sqrt(HD), BF16)
    k = dot(x, w_k[...]).astype(BF16)

    low = lax.broadcasted_iota(jnp.int32, (half, LANES), 1) < HD
    row = lax.broadcasted_iota(jnp.int32, (2 * half, half), 0)
    col = lax.broadcasted_iota(jnp.int32, (2 * half, half), 1)
    causal = jnp.where(row >= half, row - half, row) >= col
    zero = jnp.zeros((), BF16)
    jobs = []
    for g in range(pieces):
        at = slice(g * LANES, (g + 1) * LANES)
        for block in range(2):
            mine = slice(block * half, (block + 1) * half)
            qg = q[mine, at]
            both = jnp.concatenate([jnp.where(low, qg, zero), jnp.where(low, zero, qg)], axis=0)
            scores = jnp.where(causal, dot_t(both, k[mine, at]), NEG_LARGE)
            if block:
                scores = jnp.concatenate([dot_t(both, k[:half, at]), scores], axis=1)
            jobs.append((mine, at, scores))
    weights = []
    for _, _, scores in jobs:
        top = jnp.max(scores, axis=-1, keepdims=True)
        weights.append(jnp.exp(scores - top).astype(BF16))

    copies[0].wait()
    v = dot(x, w_v[...]).astype(BF16)
    heads = max(8, cols // HD)
    mask = head_mask(heads, cols)
    own_q, own_k, own_v = (part[pre_len:].astype(F32)[:1] for part in (q, k, v))
    own_score = jnp.sum(jnp.where(mask, own_q * own_k, 0.0), axis=1, keepdims=True)
    own_level = jnp.sum(jnp.where(mask, own_score, 0.0), axis=0, keepdims=True)

    ones = jnp.ones((pre_len, LANES), BF16)
    for (mine, at, _), weight in zip(jobs, weights):
        values = jnp.concatenate([v[: mine.stop, at], ones[: mine.stop]], axis=1)
        out = dot(weight, values)
        out = out[:, :LANES] / out[:, LANES:]
        ctx[mine, at] = jnp.where(low, out[:half], out[half:]).astype(BF16)

    sources = slice(None)
    if got.shape[0] > n_req:
        sources = pl.ds(pl.multiple_of(lax.axis_index("tensor") * n_req, n_req), n_req)
    is_first = lax.broadcasted_iota(jnp.int32, (TAIL, LANES), 0) == 0
    for g in range(pieces):
        at = slice(g * LANES, (g + 1) * LANES)
        level = got[sources, pieces + g, :]
        top = jnp.maximum(jnp.max(level, axis=0, keepdims=True), own_level[:, at])
        share = jnp.exp(level - top)
        own_share = jnp.exp(own_level[:, at] - top)
        numer = jnp.sum(share * got[sources, g, :], axis=0, keepdims=True) + own_share * own_v[:, at]
        denom = jnp.sum(share, axis=0, keepdims=True) + own_share
        ctx[pre_len:, at] = jnp.where(is_first, numer / denom, 0.0).astype(BF16)
    copies[1].wait()
    term[...] = dot(ctx[...], w_out[...]).astype(BF16)


def attend(rows, w_q, w_k, got, w_qkv, w_out, n_req):
    width, cols = w_q.shape
    return pl.pallas_call(
        functools.partial(attend_kernel, n_req),
        in_specs=[HBM] * 2 + [VMEM] * 4,
        out_specs=VMEM,
        out_shape=like(rows),
        scratch_shapes=[
            pltpu.VMEM((width, cols), BF16),
            pltpu.VMEM((cols, width), BF16),
            pltpu.VMEM((rows.shape[0], cols), BF16),
            pltpu.SemaphoreType.DMA((2,)),
        ],
        compiler_params=params(20),
        cost_estimate=cost(6_000_000_000),
        name="attend",
    )(in_hbm(w_qkv), in_hbm(w_out), rows, w_q, w_k, got)


def mlp_kernel(n_terms, tile, rows, *refs):
    terms = refs[:n_terms]
    gain, shift, w_up, w_down, first_ref, term = refs[n_terms:]
    units = w_up.shape[1]
    attn = terms[0][...].astype(F32)
    for other in terms[1:]:
        attn = attn + other[...].astype(F32)
    first = norm_rows(rows[...].astype(F32) + attn, gain[...], shift[...]).astype(BF16)
    first_ref[...] = first
    hidden = []
    for at in range(0, units, tile):
        hidden.append(gelu(dot(first, w_up[:, at : at + tile])).astype(BF16))
    term[...] = dot(jnp.concatenate(hidden, axis=1), w_down[...]).astype(BF16)


def mlp(rows, terms, gain, shift, w_up, w_down):
    units = w_up.shape[1]
    tile = min(512, units)
    return pl.pallas_call(
        functools.partial(mlp_kernel, len(terms), tile),
        in_specs=[VMEM] * (5 + len(terms)),
        out_specs=[VMEM] * 2,
        out_shape=[like(rows), like(rows)],
        compiler_params=params(28),
        cost_estimate=cost(),
        name="mlp",
    )(rows, *terms, gain, shift, w_up, w_down)


def finish_kernel(n_terms, first, *refs):
    terms = refs[:n_terms]
    gain, shift, pre_out, dec_out, scr = refs[n_terms:]
    mlp_sum = terms[0][...].astype(F32)
    for other in terms[1:]:
        mlp_sum = mlp_sum + other[...].astype(F32)
    total = first[...].astype(F32) + mlp_sum
    centered = total - jnp.mean(total, axis=-1, keepdims=True)
    scr[...] = centered
    var = jnp.mean(centered * centered, axis=-1, keepdims=True)
    pre_len, cols = pre_out.shape
    at = pl.ds(pl.multiple_of(lax.axis_index("tensor") * cols, LANES), cols)
    out = (scr[:, at] * lax.rsqrt(var + NORM_EPS) * gain[:, at] + shift[:, at]).astype(BF16)
    pre_out[...] = out[:pre_len]
    dec_out[...] = out[pre_len:].astype(F32)[:1].astype(BF16)


def finish(first, terms, gain, shift, cols):
    count, width = first.shape
    return pl.pallas_call(
        functools.partial(finish_kernel, len(terms)),
        in_specs=[VMEM] * (3 + len(terms)),
        out_specs=[VMEM] * 2,
        out_shape=[
            jax.ShapeDtypeStruct((count - TAIL, cols), BF16),
            jax.ShapeDtypeStruct((1, cols), BF16),
        ],
        scratch_shapes=[pltpu.VMEM((count, width), F32)],
        compiler_params=params(12),
        cost_estimate=cost(),
        name="finish",
    )(first, *terms, gain, shift)


def local(
    pre_tokens,
    dec_tokens,
    req_of,
    page_table,
    page_place,
    cache_lengths,
    cache_keys,
    cache_values,
    w_qkv,
    w_out,
    ln1_gain,
    ln1_bias,
    w_up,
    w_down,
    ln2_gain,
    ln2_bias,
):
    cols = w_qkv.shape[2]
    n_req = lax.axis_size("req")
    n_tensor = lax.axis_size("tensor")
    w_qkv = jnp.transpose(w_qkv, (1, 0, 2))
    gain1, bias1, gain2, bias2 = (
        jnp.reshape(v, (1, -1)) for v in (ln1_gain, ln1_bias, ln2_gain, ln2_bias)
    )

    def swapped(x):
        return lax.ppermute(x, "tensor", [(0, 1), (1, 0)])

    def gathered_terms(x):
        if n_tensor == 2:
            return (x, swapped(x))
        return (lax.psum(x, "tensor"),)

    if n_tensor == 2:
        chunks = (pre_tokens, swapped(pre_tokens))
    else:
        chunks = (lax.all_gather(pre_tokens, "tensor", axis=1, tiled=True),)
    lists = (req_of, page_table, page_place, cache_lengths)
    spread, w_q = start(dec_tokens, w_qkv, n_tensor * n_req)
    tokens = lax.all_to_all(spread, ("tensor", "req"), split_axis=0, concat_axis=0, tiled=True)
    sent, rows, w_k = pages(chunks, w_qkv, lists, tokens, w_q, cache_keys, cache_values, n_tensor)
    axes = ("tensor", "req") if n_tensor == 2 else "req"
    got = lax.all_to_all(sent, axes, split_axis=0, concat_axis=0, tiled=True)
    attn_term = attend(rows, w_q, w_k, got, w_qkv, w_out, n_req)
    first, mlp_term = mlp(rows, gathered_terms(attn_term), gain1, bias1, w_up, w_down)
    return tuple(finish(first, gathered_terms(mlp_term), gain2, bias2, cols))


def solution(mesh):
    in_specs = (
        P("req", "tensor"),
        P("req", "tensor"),
        P(),
        P(),
        P(),
        P(),
        P("req", None, "tensor"),
        P("req", None, "tensor"),
        P(None, None, "tensor"),
        P("tensor", None),
        P(),
        P(),
        P(None, "tensor"),
        P("tensor", None),
        P(),
        P(),
    )
    out_specs = (P("req", "tensor"), P("req", "tensor"))
    return jax.shard_map(local, mesh=mesh, in_specs=in_specs, out_specs=out_specs, check_vma=False)
```

```python
import functools
import math

import jax
import jax.numpy as jnp
from jax import lax
from jax.experimental import pallas as pl
from jax.experimental.pallas import tpu as pltpu
from jax.sharding import PartitionSpec as P

HD = 64
LANES = 128
TAIL = 16
NORM_EPS = 1e-05
NEG_LARGE = -1e30
BF16 = jnp.bfloat16
F32 = jnp.float32

VMEM = pl.BlockSpec(memory_space=pltpu.VMEM)
HBM = pl.BlockSpec(memory_space=pltpu.HBM)


def in_hbm(x):
    return pltpu.with_memory_space_constraint(x, pltpu.HBM)


def like(x):
    return jax.ShapeDtypeStruct(x.shape, x.dtype)


def params(mib):
    return pltpu.CompilerParams(vmem_limit_bytes=mib << 20)


def cost(flops=1):
    return pl.CostEstimate(flops=flops, bytes_accessed=1, transcendentals=0)


def start_all(copies):
    @pl.loop(0, jnp.where(lax.axis_index("req") >= 0, 1, 0))
    def _(_):
        for copy in copies:
            copy.start()


def dot(left, right):
    return jnp.dot(left, right, preferred_element_type=F32)


def dot_t(left, right):
    return lax.dot_general(left, right, (((1,), (1,)), ((), ())), preferred_element_type=F32)


def norm_rows(total, gain, shift):
    mean = jnp.mean(total, axis=-1, keepdims=True)
    centered = total - mean
    var = jnp.mean(centered * centered, axis=-1, keepdims=True)
    return centered * lax.rsqrt(var + NORM_EPS) * gain + shift


def gelu(x):
    return 0.5 * x * (1.0 + lax.erf(x * (1.0 / math.sqrt(2.0))))


def head_mask(rows, cols):
    head = lax.broadcasted_iota(jnp.int32, (rows, cols), 0)
    lane = lax.broadcasted_iota(jnp.int32, (rows, cols), 1)
    return lane // HD == head


def start_kernel(token_hbm, chunk_hbm, out, block, token, sems):
    pre_len = chunk_hbm.shape[0]
    fetch = pltpu.make_async_copy(token_hbm, token, sems.at[0])
    rows = pltpu.make_async_copy(chunk_hbm, block.at[pl.ds(0, pre_len)], sems.at[1])
    start_all((fetch, rows))
    fetch.wait()
    own = token[...].astype(F32)
    for r in range(out.shape[1]):
        out[:, r, :] = jnp.broadcast_to(own[:, r * LANES : (r + 1) * LANES], (out.shape[0], LANES))
    is_first = lax.broadcasted_iota(jnp.int32, (TAIL, own.shape[1]), 0) == 0
    block[pre_len:, :] = jnp.where(is_first, own, 0.0).astype(BF16)
    rows.wait()


def start(token, chunk, count):
    pre_len, cols = chunk.shape
    return pl.pallas_call(
        start_kernel,
        in_specs=[HBM] * 2,
        out_specs=[VMEM] * 2,
        out_shape=[
            jax.ShapeDtypeStruct((count, cols // LANES, LANES), F32),
            jax.ShapeDtypeStruct((pre_len + TAIL, cols), BF16),
        ],
        scratch_shapes=[pltpu.VMEM(token.shape, BF16), pltpu.SemaphoreType.DMA((2,))],
        compiler_params=params(8),
        cost_estimate=cost(),
        name="start",
    )(in_hbm(token), in_hbm(chunk))


def row_copies(blocks, count, rows, sems):
    part = lax.axis_index("tensor")
    copies = []
    for c, block in enumerate(blocks):
        wide = block.shape[1]
        offset = part * wide if c == 0 else (1 - part) * wide
        band = pl.ds(pl.multiple_of(offset, LANES), wide) if len(blocks) > 1 else slice(None)
        copies.append(pltpu.make_async_copy(block.at[pl.ds(0, count)], rows.at[:, band], sems.at[c]))
    return copies


def pages_kernel(n_tensor, values_hbm, req_of, table, place, lengths, tokens, w_q, keys, sent, values, sem):
    fetch = pltpu.make_async_copy(values_hbm, values, sem)
    start_all((fetch,))
    n_req, max_pages = table.shape
    cols = w_q.shape[1]
    pieces = cols // LANES
    pages_here, page_len = keys.shape[:2]
    heads = max(8, cols // HD)
    me = lax.axis_index("req")
    part = lax.axis_index("tensor")
    x = jnp.concatenate(
        [tokens[t * n_req : (t + 1) * n_req, r, :] for t in range(n_tensor) for r in range(pieces)],
        axis=1,
    )
    q = dot(x.astype(BF16), w_q[...]).astype(BF16).astype(F32) * (1.0 / math.sqrt(HD))

    slot_row = lax.broadcasted_iota(jnp.int32, (n_req, n_req), 0)
    slot_col = lax.broadcasted_iota(jnp.int32, (n_req, n_req), 1)
    request = jnp.sum(jnp.where(slot_row == slot_col, req_of[...], 0), axis=1, keepdims=True)
    served = request == slot_col
    length = jnp.sum(jnp.where(served, lengths[...], 0), axis=1, keepdims=True)
    ids = jnp.dot(
        served.astype(F32),
        table[...].astype(F32),
        precision=lax.Precision.HIGHEST,
        preferred_element_type=F32,
    ).astype(jnp.int32)
    at_page = lax.broadcasted_iota(jnp.int32, (n_req, max_pages), 1)
    left = length - at_page * page_len
    page_ids = lax.broadcasted_iota(jnp.int32, place.shape, 1)
    owners = []
    usable = []
    for p in range(pages_here):
        page = jnp.sum(jnp.where(place[...] == me * pages_here + p, page_ids, 0), axis=1, keepdims=True)
        hit = ids == page
        owners.append(jnp.sum(jnp.where(hit, 1.0, 0.0), axis=1, keepdims=True))
        count = jnp.sum(jnp.where(hit, left, 0), axis=1, keepdims=True)
        usable.append(jnp.sum(count, axis=0, keepdims=True))

    mask = head_mask(heads, cols)
    token = lax.broadcasted_iota(jnp.int32, (heads, page_len), 1)

    def spread(per_head):
        return jnp.sum(jnp.where(mask, per_head, 0.0), axis=0, keepdims=True)

    scores = []
    for p in range(pages_here):
        query = jnp.sum(owners[p] * q, axis=0, keepdims=True)
        query = jnp.where(mask, query, 0.0).astype(BF16)
        scores.append(jnp.where(token < usable[p], dot_t(query, keys[p]), NEG_LARGE))
    scores = jnp.concatenate(scores, axis=0)
    top = jnp.max(scores, axis=-1, keepdims=True)
    weights = jnp.exp(scores - top)
    total = jnp.sum(weights, axis=-1, keepdims=True)
    level = top + jnp.log(total)
    weights = weights.astype(BF16)
    fetch.wait()
    context = jnp.zeros((n_req, cols), F32)
    levels = (1.0 - sum(owners)) * jnp.full((n_req, cols), NEG_LARGE, F32)
    for p in range(pages_here):
        at = slice(p * heads, (p + 1) * heads)
        context = context + owners[p] * spread(dot(weights[at], values[p]) / total[at])
        levels = levels + owners[p] * spread(level[at])
    to = pl.ds(pl.multiple_of(part * n_req, n_req), n_req) if n_tensor == 2 else slice(None)
    if n_tensor == 2:
        sent[...] = jnp.zeros(sent.shape, F32)
    for r in range(pieces):
        sent[to, r, :] = context[:, r * LANES : (r + 1) * LANES]
        sent[to, pieces + r, :] = levels[:, r * LANES : (r + 1) * LANES]


def pages(lists, tokens, w_q, keys, values, n_tensor):
    cols = w_q.shape[1]
    n_req = lists[0].shape[0]
    twice = 2 * (cols // LANES)
    req_of, table, place, lengths = lists
    return pl.pallas_call(
        functools.partial(pages_kernel, n_tensor),
        in_specs=[HBM] + [VMEM] * 7,
        out_specs=VMEM,
        scratch_shapes=[pltpu.VMEM(values.shape, BF16), pltpu.SemaphoreType.DMA],
        out_shape=jax.ShapeDtypeStruct((n_req * (2 if n_tensor == 2 else 1), twice, LANES), F32),
        compiler_params=params(12),
        cost_estimate=cost(),
        name="pages",
    )(
        in_hbm(values),
        req_of.reshape(1, -1),
        table,
        place.reshape(1, -1),
        lengths.reshape(1, -1),
        tokens,
        w_q,
        keys,
    )


def attend_kernel(n_blocks, w_qkv_hbm, w_out_hbm, *refs):
    blocks = refs[:n_blocks]
    term, dec_row, own, w_q, rows, w_kv, w_out, ctx, sems = refs[n_blocks:]
    count = rows.shape[0]
    pre_len = count - TAIL
    inputs = row_copies(blocks, count, rows, sems)
    sources = (w_qkv_hbm.at[0], w_qkv_hbm.at[1], w_qkv_hbm.at[2], w_out_hbm)
    targets = (w_q, w_kv.at[0], w_kv.at[1], w_out)
    copies = [
        pltpu.make_async_copy(source, target, sems.at[n_blocks + i])
        for i, (source, target) in enumerate(zip(sources, targets))
    ]
    start_all((*inputs, *copies))
    for copy in inputs:
        copy.wait()
    dec_row[...] = rows[pre_len:, :]
    cols = w_q.shape[1]
    pieces = cols // LANES
    half = pre_len // 2
    x = rows[...]
    copies[0].wait()
    q = dot(x, w_q[...]).astype(BF16) * jnp.asarray(1.0 / math.sqrt(HD), BF16)
    copies[1].wait()
    k = dot(x, w_kv[0]).astype(BF16)

    low = lax.broadcasted_iota(jnp.int32, (half, LANES), 1) < HD
    row = lax.broadcasted_iota(jnp.int32, (2 * half, half), 0)
    col = lax.broadcasted_iota(jnp.int32, (2 * half, half), 1)
    causal = jnp.where(row >= half, row - half, row) >= col
    zero = jnp.zeros((), BF16)
    jobs = []
    for g in range(pieces):
        at = slice(g * LANES, (g + 1) * LANES)
        for block in range(2):
            mine = slice(block * half, (block + 1) * half)
            qg = q[mine, at]
            both = jnp.concatenate([jnp.where(low, qg, zero), jnp.where(low, zero, qg)], axis=0)
            scores = jnp.where(causal, dot_t(both, k[mine, at]), NEG_LARGE)
            if block:
                scores = jnp.concatenate([dot_t(both, k[:half, at]), scores], axis=1)
            jobs.append((mine, at, scores))
    weights = []
    for _, _, scores in jobs:
        top = jnp.max(scores, axis=-1, keepdims=True)
        weights.append(jnp.exp(scores - top).astype(BF16))

    copies[2].wait()
    v = dot(x, w_kv[1]).astype(BF16)
    heads = max(8, cols // HD)
    mask = head_mask(heads, cols)
    own_q, own_k, own_v = (part[pre_len:].astype(F32)[:1] for part in (q, k, v))
    own_score = jnp.sum(jnp.where(mask, own_q * own_k, 0.0), axis=1, keepdims=True)
    own[0:1, :] = own_v
    own[1:2, :] = jnp.sum(jnp.where(mask, own_score, 0.0), axis=0, keepdims=True)

    ones = jnp.ones((pre_len, LANES), BF16)
    for (mine, at, _), weight in zip(jobs, weights):
        values = jnp.concatenate([v[: mine.stop, at], ones[: mine.stop]], axis=1)
        out = dot(weight, values)
        out = out[:, :LANES] / out[:, LANES:]
        ctx[mine, at] = jnp.where(low, out[:half], out[half:]).astype(BF16)

    copies[3].wait()
    term[...] = dot(ctx[...], w_out[...]).astype(BF16)


def attend(blocks, w_qkv, w_out):
    width, cols = w_qkv.shape[1:]
    count = blocks[0].shape[0]
    return pl.pallas_call(
        functools.partial(attend_kernel, len(blocks)),
        in_specs=[HBM] * 2 + [VMEM] * len(blocks),
        out_specs=[VMEM] * 4,
        out_shape=[
            jax.ShapeDtypeStruct((count - TAIL, width), BF16),
            jax.ShapeDtypeStruct((TAIL, width), BF16),
            jax.ShapeDtypeStruct((2, cols), F32),
            jax.ShapeDtypeStruct((width, cols), BF16),
        ],
        scratch_shapes=[
            pltpu.VMEM((count, width), BF16),
            pltpu.VMEM((2, width, cols), BF16),
            pltpu.VMEM(w_out.shape, BF16),
            pltpu.VMEM((count - TAIL, cols), BF16),
            pltpu.SemaphoreType.DMA((4 + len(blocks),)),
        ],
        compiler_params=params(20),
        cost_estimate=cost(),
        name="attend",
    )(in_hbm(w_qkv), in_hbm(w_out), *blocks)


def join_kernel(n_req, got, own, w_out, term):
    cols = own.shape[1]
    pieces = cols // LANES
    sources = slice(None)
    if got.shape[0] > n_req:
        sources = pl.ds(pl.multiple_of(lax.axis_index("tensor") * n_req, n_req), n_req)
    context = []
    for g in range(pieces):
        at = slice(g * LANES, (g + 1) * LANES)
        level = got[sources, pieces + g, :]
        own_level = own[1:2, at]
        top = jnp.maximum(jnp.max(level, axis=0, keepdims=True), own_level)
        share = jnp.exp(level - top)
        own_share = jnp.exp(own_level - top)
        numer = jnp.sum(share * got[sources, g, :], axis=0, keepdims=True) + own_share * own[0:1, at]
        context.append(numer / (jnp.sum(share, axis=0, keepdims=True) + own_share))
    context = jnp.broadcast_to(jnp.concatenate(context, axis=1), (TAIL, cols))
    term[...] = dot(context.astype(BF16), w_out[...]).astype(BF16)


def join(got, own, w_out, n_req):
    return pl.pallas_call(
        functools.partial(join_kernel, n_req),
        in_specs=[VMEM] * 3,
        out_specs=VMEM,
        out_shape=jax.ShapeDtypeStruct((TAIL, w_out.shape[1]), BF16),
        compiler_params=params(8),
        cost_estimate=cost(6_000_000_000),
        name="join",
    )(got, own, w_out)


def first_rows(rows, terms, gain, shift):
    attn = 0.0
    for group in terms:
        attn = attn + jnp.concatenate([part[...].astype(F32) for part in group], axis=0)
    return norm_rows(rows.astype(F32) + attn, gain[...], shift[...]).astype(BF16)


def split_refs(refs, counts):
    groups = []
    for count in counts:
        groups.append(refs[:count])
        refs = refs[count:]
    return groups, refs


def mlp_kernel(n_blocks, counts, tile, w_up_hbm, w_down_hbm, *refs):
    blocks = refs[:n_blocks]
    terms, refs = split_refs(refs[n_blocks:], counts)
    gain, shift, first_ref, term, rows, w_up, w_down, sems = refs
    units = w_up.shape[1]
    steps = range(0, units, tile)
    inputs = row_copies(blocks, rows.shape[0], rows, sems)
    ups, downs = [], []
    for i, unit in enumerate(steps):
        part = pl.ds(unit, tile)
        at = n_blocks + 2 * i
        ups.append(pltpu.make_async_copy(w_up_hbm.at[:, part], w_up.at[:, part], sems.at[at]))
        downs.append(pltpu.make_async_copy(w_down_hbm.at[part], w_down.at[part], sems.at[at + 1]))
    start_all((*inputs, *ups, *downs))
    for copy in inputs:
        copy.wait()
    first = first_rows(rows[...], terms, gain, shift)
    first_ref[...] = first
    hidden = []
    for unit, copy in zip(steps, ups):
        copy.wait()
        hidden.append(gelu(dot(first, w_up[:, unit : unit + tile])).astype(BF16))
    total = 0.0
    for i, copy in enumerate(downs):
        copy.wait()
        total = total + dot(hidden[i], w_down[i * tile : (i + 1) * tile, :])
    term[...] = total.astype(BF16)


def mlp(blocks, terms, gain, shift, w_up, w_down):
    counts = [len(group) for group in terms]
    count = blocks[0].shape[0] - TAIL
    width, units = w_up.shape
    tile = min(512, units)
    return pl.pallas_call(
        functools.partial(mlp_kernel, len(blocks), counts, tile),
        in_specs=[HBM] * 2 + [VMEM] * (2 + len(blocks) + sum(counts)),
        out_specs=[VMEM] * 2,
        out_shape=[jax.ShapeDtypeStruct((count, width), BF16)] * 2,
        scratch_shapes=[
            pltpu.VMEM((count, width), BF16),
            pltpu.VMEM(w_up.shape, BF16),
            pltpu.VMEM(w_down.shape, BF16),
            pltpu.SemaphoreType.DMA((len(blocks) + 2 * (units // tile),)),
        ],
        compiler_params=params(28),
        cost_estimate=cost(),
        name="pre_mlp",
    )(in_hbm(w_up), in_hbm(w_down), *blocks, *(part for group in terms for part in group), gain, shift)


def up_kernel(counts, rows, *refs):
    terms, (gain, shift, w_up, first_ref, hidden) = split_refs(refs, counts)
    first = first_rows(rows[...], terms, gain, shift)
    first_ref[...] = first
    hidden[...] = gelu(dot(first, w_up[...])).astype(BF16)


def up(rows, terms, gain, shift, w_up):
    counts = [len(group) for group in terms]
    width, units = w_up.shape
    return pl.pallas_call(
        functools.partial(up_kernel, counts),
        in_specs=[VMEM] * (4 + sum(counts)),
        out_specs=[VMEM] * 2,
        out_shape=[jax.ShapeDtypeStruct((TAIL, width), BF16), jax.ShapeDtypeStruct((TAIL, units), BF16)],
        compiler_params=params(20),
        cost_estimate=cost(6_000_000_000),
        name="dec_up",
    )(rows, *(part for group in terms for part in group), gain, shift, w_up)


def down_kernel(hidden, w_down, term):
    term[...] = dot(hidden[...], w_down[...]).astype(BF16)


def down(hidden, w_down):
    return pl.pallas_call(
        down_kernel,
        in_specs=[VMEM] * 2,
        out_specs=VMEM,
        out_shape=jax.ShapeDtypeStruct((hidden.shape[0], w_down.shape[1]), BF16),
        compiler_params=params(20),
        cost_estimate=cost(),
        name="dec_down",
    )(hidden, w_down)


def finish_kernel(n_terms, first, *refs):
    terms = refs[:n_terms]
    gain, shift, out, scr = refs[n_terms:]
    mlp_sum = terms[0][...].astype(F32)
    for other in terms[1:]:
        mlp_sum = mlp_sum + other[...].astype(F32)
    total = first[...].astype(F32) + mlp_sum
    centered = total - jnp.mean(total, axis=-1, keepdims=True)
    scr[...] = centered
    var = jnp.mean(centered * centered, axis=-1, keepdims=True)
    kept, cols = out.shape
    at = pl.ds(pl.multiple_of(lax.axis_index("tensor") * cols, LANES), cols)
    normed = scr[:, at] * lax.rsqrt(var + NORM_EPS) * gain[:, at] + shift[:, at]
    out[...] = normed[:kept].astype(BF16)


def finish(first, terms, gain, shift, kept, cols, name):
    return pl.pallas_call(
        functools.partial(finish_kernel, len(terms)),
        in_specs=[VMEM] * (3 + len(terms)),
        out_specs=VMEM,
        out_shape=jax.ShapeDtypeStruct((kept, cols), BF16),
        scratch_shapes=[pltpu.VMEM(first.shape, F32)],
        compiler_params=params(12),
        cost_estimate=cost(),
        name=name,
    )(first, *terms, gain, shift)


def local(
    pre_tokens,
    dec_tokens,
    req_of,
    page_table,
    page_place,
    cache_lengths,
    cache_keys,
    cache_values,
    w_qkv,
    w_out,
    ln1_gain,
    ln1_bias,
    w_up,
    w_down,
    ln2_gain,
    ln2_bias,
):
    cols = w_qkv.shape[2]
    n_req = lax.axis_size("req")
    n_tensor = lax.axis_size("tensor")
    w_qkv = jnp.transpose(w_qkv, (1, 0, 2))
    gain1, bias1, gain2, bias2 = (
        jnp.reshape(v, (1, -1)) for v in (ln1_gain, ln1_bias, ln2_gain, ln2_bias)
    )

    def swapped(x):
        return lax.ppermute(x, "tensor", [(0, 1), (1, 0)])

    def gathered_terms(x, cuts=1):
        if n_tensor == 2:
            step = x.shape[0] // cuts
            return ((x,), tuple(swapped(x[i * step : (i + 1) * step]) for i in range(cuts)))
        return ((lax.psum(x, "tensor"),),)

    pre_len = pre_tokens.shape[0]
    lists = (req_of, page_table, page_place, cache_lengths)
    spread, block = start(dec_tokens, pre_tokens, n_tensor * n_req)
    tokens = lax.all_to_all(spread, ("tensor", "req"), split_axis=0, concat_axis=0, tiled=True)
    if n_tensor == 2:
        blocks = (block, swapped(block))
    else:
        blocks = (lax.all_gather(block, "tensor", axis=1, tiled=True),)
    pre_term, dec_row, own, w_q = attend(blocks, w_qkv, w_out)
    tokens, own = lax.optimization_barrier((tokens, own))
    sent = pages(lists, tokens, w_q, cache_keys, cache_values, n_tensor)
    sent, pre_term = lax.optimization_barrier((sent, pre_term))
    axes = ("tensor", "req") if n_tensor == 2 else "req"
    got = lax.all_to_all(sent, axes, split_axis=0, concat_axis=0, tiled=True)
    pre_first, pre_mlp = mlp(blocks, gathered_terms(pre_term), gain1, bias1, w_up, w_down)
    own, pre_mlp = lax.optimization_barrier((own, pre_mlp))
    dec_term = join(got, own, w_out, n_req)
    dec_term, pre_mlp = lax.optimization_barrier((dec_term, pre_mlp))
    pre_groups = gathered_terms(pre_mlp)
    dec_first, hidden = up(dec_row, gathered_terms(dec_term), gain1, bias1, w_up)
    dec_mlp = down(hidden, w_down)
    pre_out = finish(pre_first, [group[0] for group in pre_groups], gain2, bias2, pre_len, cols, "pre_norm")
    dec_first, pre_out = lax.optimization_barrier((dec_first, pre_out))
    dec_groups = gathered_terms(dec_mlp)
    dec_out = finish(dec_first, [group[0] for group in dec_groups], gain2, bias2, 1, cols, "dec_norm")
    return (pre_out, dec_out)


def solution(mesh):
    in_specs = (
        P("req", "tensor"),
        P("req", "tensor"),
        P(),
        P(),
        P(),
        P(),
        P("req", None, "tensor"),
        P("req", None, "tensor"),
        P(None, None, "tensor"),
        P("tensor", None),
        P(),
        P(),
        P(None, "tensor"),
        P("tensor", None),
        P(),
        P(),
    )
    out_specs = (P("req", "tensor"), P("req", "tensor"))
    return jax.shard_map(local, mesh=mesh, in_specs=in_specs, out_specs=out_specs, check_vma=False)
```

```python
import functools
import math

import jax
import jax.numpy as jnp
from jax import lax
from jax.experimental import pallas as pl
from jax.experimental.pallas import tpu as pltpu
from jax.sharding import PartitionSpec as P

HD = 64
LANES = 128
TAIL = 16
NORM_EPS = 1e-05
NEG_LARGE = -1e30
BF16 = jnp.bfloat16
F32 = jnp.float32

VMEM = pl.BlockSpec(memory_space=pltpu.VMEM)
HBM = pl.BlockSpec(memory_space=pltpu.HBM)


def in_hbm(x):
    return pltpu.with_memory_space_constraint(x, pltpu.HBM)


def like(x):
    return jax.ShapeDtypeStruct(x.shape, x.dtype)


def params(mib):
    return pltpu.CompilerParams(vmem_limit_bytes=mib << 20)


def cost(flops=1):
    return pl.CostEstimate(flops=flops, bytes_accessed=1, transcendentals=0)


def start_all(copies):
    @pl.loop(0, jnp.where(lax.axis_index("req") >= 0, 1, 0))
    def _(_):
        for copy in copies:
            copy.start()


def dot(left, right):
    return jnp.dot(left, right, preferred_element_type=F32)


def dot_t(left, right):
    return lax.dot_general(left, right, (((1,), (1,)), ((), ())), preferred_element_type=F32)


def norm_rows(total, gain, shift):
    mean = jnp.mean(total, axis=-1, keepdims=True)
    centered = total - mean
    var = jnp.mean(centered * centered, axis=-1, keepdims=True)
    return centered * lax.rsqrt(var + NORM_EPS) * gain + shift


def gelu(x):
    return 0.5 * x * (1.0 + lax.erf(x * (1.0 / math.sqrt(2.0))))


def head_mask(rows, cols):
    head = lax.broadcasted_iota(jnp.int32, (rows, cols), 0)
    lane = lax.broadcasted_iota(jnp.int32, (rows, cols), 1)
    return lane // HD == head


def start_kernel(token_hbm, chunk_hbm, w_qkv_hbm, out_hbm, block, w_q, out, token, sems):
    pre_len = chunk_hbm.shape[0]
    fetch = pltpu.make_async_copy(token_hbm, token, sems.at[0])
    rows = pltpu.make_async_copy(chunk_hbm, block.at[pl.ds(0, pre_len)], sems.at[1])
    weights = pltpu.make_async_copy(w_qkv_hbm.at[0], w_q, sems.at[3])
    start_all((fetch, rows, weights))
    fetch.wait()
    own = token[...].astype(F32)
    for r in range(out.shape[1]):
        out[:, r, :] = jnp.broadcast_to(own[:, r * LANES : (r + 1) * LANES], (out.shape[0], LANES))
    spread = pltpu.make_async_copy(out, out_hbm, sems.at[2])
    start_all((spread,))
    is_first = lax.broadcasted_iota(jnp.int32, (TAIL, own.shape[1]), 0) == 0
    block[pre_len:, :] = jnp.where(is_first, own, 0.0).astype(BF16)
    rows.wait()
    spread.wait()
    weights.wait()


def start(token, chunk, w_qkv, count):
    pre_len, cols = chunk.shape
    return pl.pallas_call(
        start_kernel,
        in_specs=[HBM] * 3,
        out_specs=[HBM, VMEM, VMEM],
        out_shape=[
            pltpu.HBM((count, cols // LANES, LANES), F32),
            jax.ShapeDtypeStruct((pre_len + TAIL, cols), BF16),
            jax.ShapeDtypeStruct(w_qkv.shape[1:], BF16),
        ],
        scratch_shapes=[
            pltpu.VMEM((count, cols // LANES, LANES), F32),
            pltpu.VMEM(token.shape, BF16),
            pltpu.SemaphoreType.DMA((4,)),
        ],
        compiler_params=params(8),
        cost_estimate=cost(),
        name="start",
    )(in_hbm(token), in_hbm(chunk), in_hbm(w_qkv))


def row_copies(blocks, count, rows, sems):
    part = lax.axis_index("tensor")
    copies = []
    for c, block in enumerate(blocks):
        wide = block.shape[1]
        offset = part * wide if c == 0 else (1 - part) * wide
        band = pl.ds(pl.multiple_of(offset, LANES), wide) if len(blocks) > 1 else slice(None)
        copies.append(pltpu.make_async_copy(block.at[pl.ds(0, count)], rows.at[:, band], sems.at[c]))
    return copies


def pages_kernel(n_tensor, values_hbm, req_of, table, place, lengths, tokens, w_q, keys, sent, values, sem):
    fetch = pltpu.make_async_copy(values_hbm, values, sem)
    start_all((fetch,))
    n_req, max_pages = table.shape
    cols = w_q.shape[1]
    pieces = cols // LANES
    pages_here, page_len = keys.shape[:2]
    heads = max(8, cols // HD)
    me = lax.axis_index("req")
    part = lax.axis_index("tensor")
    x = jnp.concatenate(
        [tokens[t * n_req : (t + 1) * n_req, r, :] for t in range(n_tensor) for r in range(pieces)],
        axis=1,
    )
    q = dot(x.astype(BF16), w_q[...]).astype(BF16).astype(F32) * (1.0 / math.sqrt(HD))

    slot_row = lax.broadcasted_iota(jnp.int32, (n_req, n_req), 0)
    slot_col = lax.broadcasted_iota(jnp.int32, (n_req, n_req), 1)
    request = jnp.sum(jnp.where(slot_row == slot_col, req_of[...], 0), axis=1, keepdims=True)
    served = request == slot_col
    length = jnp.sum(jnp.where(served, lengths[...], 0), axis=1, keepdims=True)
    ids = jnp.dot(
        served.astype(F32),
        table[...].astype(F32),
        precision=lax.Precision.HIGHEST,
        preferred_element_type=F32,
    ).astype(jnp.int32)
    at_page = lax.broadcasted_iota(jnp.int32, (n_req, max_pages), 1)
    left = length - at_page * page_len
    page_ids = lax.broadcasted_iota(jnp.int32, place.shape, 1)
    owners = []
    usable = []
    for p in range(pages_here):
        page = jnp.sum(jnp.where(place[...] == me * pages_here + p, page_ids, 0), axis=1, keepdims=True)
        hit = ids == page
        owners.append(jnp.sum(jnp.where(hit, 1.0, 0.0), axis=1, keepdims=True))
        count = jnp.sum(jnp.where(hit, left, 0), axis=1, keepdims=True)
        usable.append(jnp.sum(count, axis=0, keepdims=True))

    mask = head_mask(heads, cols)
    token = lax.broadcasted_iota(jnp.int32, (heads, page_len), 1)

    def spread(per_head):
        return jnp.sum(jnp.where(mask, per_head, 0.0), axis=0, keepdims=True)

    scores = []
    for p in range(pages_here):
        query = jnp.sum(owners[p] * q, axis=0, keepdims=True)
        query = jnp.where(mask, query, 0.0).astype(BF16)
        scores.append(jnp.where(token < usable[p], dot_t(query, keys[p]), NEG_LARGE))
    scores = jnp.concatenate(scores, axis=0)
    top = jnp.max(scores, axis=-1, keepdims=True)
    weights = jnp.exp(scores - top)
    total = jnp.sum(weights, axis=-1, keepdims=True)
    level = top + jnp.log(total)
    weights = weights.astype(BF16)
    fetch.wait()
    context = jnp.zeros((n_req, cols), F32)
    levels = (1.0 - sum(owners)) * jnp.full((n_req, cols), NEG_LARGE, F32)
    for p in range(pages_here):
        at = slice(p * heads, (p + 1) * heads)
        context = context + owners[p] * spread(dot(weights[at], values[p]) / total[at])
        levels = levels + owners[p] * spread(level[at])
    to = pl.ds(pl.multiple_of(part * n_req, n_req), n_req) if n_tensor == 2 else slice(None)
    if n_tensor == 2:
        sent[...] = jnp.zeros(sent.shape, F32)
    for r in range(pieces):
        sent[to, r, :] = context[:, r * LANES : (r + 1) * LANES]
        sent[to, pieces + r, :] = levels[:, r * LANES : (r + 1) * LANES]


def pages(lists, tokens, w_q, keys, values, n_tensor):
    cols = w_q.shape[1]
    n_req = lists[0].shape[0]
    twice = 2 * (cols // LANES)
    req_of, table, place, lengths = lists
    return pl.pallas_call(
        functools.partial(pages_kernel, n_tensor),
        in_specs=[HBM] + [VMEM] * 7,
        out_specs=VMEM,
        scratch_shapes=[pltpu.VMEM(values.shape, BF16), pltpu.SemaphoreType.DMA],
        out_shape=jax.ShapeDtypeStruct((n_req * (2 if n_tensor == 2 else 1), twice, LANES), F32),
        compiler_params=params(12),
        cost_estimate=cost(),
        name="pages",
    )(
        in_hbm(values),
        req_of.reshape(1, -1),
        table,
        place.reshape(1, -1),
        lengths.reshape(1, -1),
        tokens,
        w_q,
        keys,
    )


def attend_kernel(n_blocks, w_qkv_hbm, w_out_hbm, w_q, *refs):
    blocks = refs[:n_blocks]
    term, dec_row, own, rows, w_kv, w_out, ctx, sems = refs[n_blocks:]
    count = rows.shape[0]
    pre_len = count - TAIL
    inputs = row_copies(blocks, count, rows, sems)
    sources = (w_qkv_hbm.at[1], w_qkv_hbm.at[2], w_out_hbm)
    targets = (w_kv.at[0], w_kv.at[1], w_out)
    copies = [
        pltpu.make_async_copy(source, target, sems.at[n_blocks + i])
        for i, (source, target) in enumerate(zip(sources, targets))
    ]
    start_all((*inputs, *copies))
    for copy in inputs:
        copy.wait()
    dec_row[...] = rows[pre_len:, :]
    cols = w_q.shape[1]
    pieces = cols // LANES
    half = pre_len // 2
    x = rows[...]
    q = dot(x, w_q[...]).astype(BF16) * jnp.asarray(1.0 / math.sqrt(HD), BF16)
    copies[0].wait()
    k = dot(x, w_kv[0]).astype(BF16)

    low = lax.broadcasted_iota(jnp.int32, (half, LANES), 1) < HD
    row = lax.broadcasted_iota(jnp.int32, (2 * half, half), 0)
    col = lax.broadcasted_iota(jnp.int32, (2 * half, half), 1)
    causal = jnp.where(row >= half, row - half, row) >= col
    zero = jnp.zeros((), BF16)
    jobs = []
    for g in range(pieces):
        at = slice(g * LANES, (g + 1) * LANES)
        for block in range(2):
            mine = slice(block * half, (block + 1) * half)
            qg = q[mine, at]
            both = jnp.concatenate([jnp.where(low, qg, zero), jnp.where(low, zero, qg)], axis=0)
            scores = jnp.where(causal, dot_t(both, k[mine, at]), NEG_LARGE)
            if block:
                scores = jnp.concatenate([dot_t(both, k[:half, at]), scores], axis=1)
            jobs.append((mine, at, scores))
    weights = []
    for _, _, scores in jobs:
        top = jnp.max(scores, axis=-1, keepdims=True)
        weights.append(jnp.exp(scores - top).astype(BF16))

    copies[1].wait()
    v = dot(x, w_kv[1]).astype(BF16)
    heads = max(8, cols // HD)
    mask = head_mask(heads, cols)
    own_q, own_k, own_v = (part[pre_len:].astype(F32)[:1] for part in (q, k, v))
    own_score = jnp.sum(jnp.where(mask, own_q * own_k, 0.0), axis=1, keepdims=True)
    own[0:1, :] = own_v
    own[1:2, :] = jnp.sum(jnp.where(mask, own_score, 0.0), axis=0, keepdims=True)

    ones = jnp.ones((pre_len, LANES), BF16)
    for (mine, at, _), weight in zip(jobs, weights):
        values = jnp.concatenate([v[: mine.stop, at], ones[: mine.stop]], axis=1)
        out = dot(weight, values)
        out = out[:, :LANES] / out[:, LANES:]
        ctx[mine, at] = jnp.where(low, out[:half], out[half:]).astype(BF16)

    copies[2].wait()
    term[...] = dot(ctx[...], w_out[...]).astype(BF16)


def attend(blocks, w_q, w_qkv, w_out):
    width, cols = w_qkv.shape[1:]
    count = blocks[0].shape[0]
    return pl.pallas_call(
        functools.partial(attend_kernel, len(blocks)),
        in_specs=[HBM] * 2 + [VMEM] * (1 + len(blocks)),
        out_specs=[VMEM] * 3,
        out_shape=[
            jax.ShapeDtypeStruct((count - TAIL, width), BF16),
            jax.ShapeDtypeStruct((TAIL, width), BF16),
            jax.ShapeDtypeStruct((2, cols), F32),
        ],
        scratch_shapes=[
            pltpu.VMEM((count, width), BF16),
            pltpu.VMEM((2, width, cols), BF16),
            pltpu.VMEM(w_out.shape, BF16),
            pltpu.VMEM((count - TAIL, cols), BF16),
            pltpu.SemaphoreType.DMA((3 + len(blocks),)),
        ],
        compiler_params=params(20),
        cost_estimate=cost(),
        name="attend",
    )(in_hbm(w_qkv), in_hbm(w_out), w_q, *blocks)


def join_kernel(n_req, got, own, w_out, term):
    cols = own.shape[1]
    pieces = cols // LANES
    sources = slice(None)
    if got.shape[0] > n_req:
        sources = pl.ds(pl.multiple_of(lax.axis_index("tensor") * n_req, n_req), n_req)
    context = []
    for g in range(pieces):
        at = slice(g * LANES, (g + 1) * LANES)
        level = got[sources, pieces + g, :]
        own_level = own[1:2, at]
        top = jnp.maximum(jnp.max(level, axis=0, keepdims=True), own_level)
        share = jnp.exp(level - top)
        own_share = jnp.exp(own_level - top)
        numer = jnp.sum(share * got[sources, g, :], axis=0, keepdims=True) + own_share * own[0:1, at]
        context.append(numer / (jnp.sum(share, axis=0, keepdims=True) + own_share))
    context = jnp.broadcast_to(jnp.concatenate(context, axis=1), (TAIL, cols))
    term[...] = dot(context.astype(BF16), w_out[...]).astype(BF16)


def join(got, own, w_out, n_req):
    return pl.pallas_call(
        functools.partial(join_kernel, n_req),
        in_specs=[VMEM] * 3,
        out_specs=VMEM,
        out_shape=jax.ShapeDtypeStruct((TAIL, w_out.shape[1]), BF16),
        compiler_params=params(8),
        cost_estimate=cost(6_000_000_000),
        name="join",
    )(got, own, w_out)


def first_rows(rows, terms, gain, shift):
    attn = 0.0
    for group in terms:
        attn = attn + jnp.concatenate([part[...].astype(F32) for part in group], axis=0)
    return norm_rows(rows.astype(F32) + attn, gain[...], shift[...]).astype(BF16)


def split_refs(refs, counts):
    groups = []
    for count in counts:
        groups.append(refs[:count])
        refs = refs[count:]
    return groups, refs


def mlp_kernel(n_blocks, counts, tile, w_up_hbm, w_down_hbm, *refs):
    blocks = refs[:n_blocks]
    terms, refs = split_refs(refs[n_blocks:], counts)
    gain, shift, first_ref, term, rows, w_up, w_down, sems = refs
    units = w_up.shape[1]
    steps = range(0, units, tile)
    inputs = row_copies(blocks, rows.shape[0], rows, sems)
    ups, downs = [], []
    for i, unit in enumerate(steps):
        part = pl.ds(unit, tile)
        at = n_blocks + 2 * i
        ups.append(pltpu.make_async_copy(w_up_hbm.at[:, part], w_up.at[:, part], sems.at[at]))
        downs.append(pltpu.make_async_copy(w_down_hbm.at[part], w_down.at[part], sems.at[at + 1]))
    start_all((*inputs, *ups, *downs))
    for copy in inputs:
        copy.wait()
    first = first_rows(rows[...], terms, gain, shift)
    first_ref[...] = first
    hidden = []
    for unit, copy in zip(steps, ups):
        copy.wait()
        hidden.append(gelu(dot(first, w_up[:, unit : unit + tile])).astype(BF16))
    total = 0.0
    for i, copy in enumerate(downs):
        copy.wait()
        total = total + dot(hidden[i], w_down[i * tile : (i + 1) * tile, :])
    term[...] = total.astype(BF16)


def mlp(blocks, terms, gain, shift, w_up, w_down):
    counts = [len(group) for group in terms]
    count = blocks[0].shape[0] - TAIL
    width, units = w_up.shape
    tile = min(512, units)
    return pl.pallas_call(
        functools.partial(mlp_kernel, len(blocks), counts, tile),
        in_specs=[HBM] * 2 + [VMEM] * (2 + len(blocks) + sum(counts)),
        out_specs=[VMEM] * 2,
        out_shape=[jax.ShapeDtypeStruct((count, width), BF16)] * 2,
        scratch_shapes=[
            pltpu.VMEM((count, width), BF16),
            pltpu.VMEM(w_up.shape, BF16),
            pltpu.VMEM(w_down.shape, BF16),
            pltpu.SemaphoreType.DMA((len(blocks) + 2 * (units // tile),)),
        ],
        compiler_params=params(28),
        cost_estimate=cost(),
        name="pre_mlp",
    )(in_hbm(w_up), in_hbm(w_down), *blocks, *(part for group in terms for part in group), gain, shift)


def up_kernel(counts, rows, *refs):
    terms, (gain, shift, w_up, first_ref, hidden) = split_refs(refs, counts)
    first = first_rows(rows[...], terms, gain, shift)
    first_ref[...] = first
    hidden[...] = gelu(dot(first, w_up[...])).astype(BF16)


def up(rows, terms, gain, shift, w_up):
    counts = [len(group) for group in terms]
    width, units = w_up.shape
    return pl.pallas_call(
        functools.partial(up_kernel, counts),
        in_specs=[VMEM] * (4 + sum(counts)),
        out_specs=[VMEM] * 2,
        out_shape=[jax.ShapeDtypeStruct((TAIL, width), BF16), jax.ShapeDtypeStruct((TAIL, units), BF16)],
        compiler_params=params(20),
        cost_estimate=cost(6_000_000_000),
        name="dec_up",
    )(rows, *(part for group in terms for part in group), gain, shift, w_up)


def down_kernel(hidden, w_down, term):
    term[...] = dot(hidden[...], w_down[...]).astype(BF16)


def down(hidden, w_down):
    return pl.pallas_call(
        down_kernel,
        in_specs=[VMEM] * 2,
        out_specs=VMEM,
        out_shape=jax.ShapeDtypeStruct((hidden.shape[0], w_down.shape[1]), BF16),
        compiler_params=params(20),
        cost_estimate=cost(),
        name="dec_down",
    )(hidden, w_down)


def finish_kernel(n_terms, first, *refs):
    terms = refs[:n_terms]
    gain, shift, out, scr = refs[n_terms:]
    mlp_sum = terms[0][...].astype(F32)
    for other in terms[1:]:
        mlp_sum = mlp_sum + other[...].astype(F32)
    total = first[...].astype(F32) + mlp_sum
    centered = total - jnp.mean(total, axis=-1, keepdims=True)
    scr[...] = centered
    var = jnp.mean(centered * centered, axis=-1, keepdims=True)
    kept, cols = out.shape
    at = pl.ds(pl.multiple_of(lax.axis_index("tensor") * cols, LANES), cols)
    normed = scr[:, at] * lax.rsqrt(var + NORM_EPS) * gain[:, at] + shift[:, at]
    out[...] = normed[:kept].astype(BF16)


def finish(first, terms, gain, shift, kept, cols, name):
    return pl.pallas_call(
        functools.partial(finish_kernel, len(terms)),
        in_specs=[VMEM] * (3 + len(terms)),
        out_specs=VMEM,
        out_shape=jax.ShapeDtypeStruct((kept, cols), BF16),
        scratch_shapes=[pltpu.VMEM(first.shape, F32)],
        compiler_params=params(12),
        cost_estimate=cost(),
        name=name,
    )(first, *terms, gain, shift)


def local(
    pre_tokens,
    dec_tokens,
    req_of,
    page_table,
    page_place,
    cache_lengths,
    cache_keys,
    cache_values,
    w_qkv,
    w_out,
    ln1_gain,
    ln1_bias,
    w_up,
    w_down,
    ln2_gain,
    ln2_bias,
):
    cols = w_qkv.shape[2]
    n_req = lax.axis_size("req")
    n_tensor = lax.axis_size("tensor")
    w_qkv = jnp.transpose(w_qkv, (1, 0, 2))
    gain1, bias1, gain2, bias2 = (
        jnp.reshape(v, (1, -1)) for v in (ln1_gain, ln1_bias, ln2_gain, ln2_bias)
    )

    def swapped(x):
        return lax.ppermute(x, "tensor", [(0, 1), (1, 0)])

    def gathered_terms(x, cuts=1):
        if n_tensor == 2:
            step = x.shape[0] // cuts
            return ((x,), tuple(swapped(x[i * step : (i + 1) * step]) for i in range(cuts)))
        return ((lax.psum(x, "tensor"),),)

    pre_len = pre_tokens.shape[0]
    lists = (req_of, page_table, page_place, cache_lengths)
    spread, block, w_q = start(dec_tokens, pre_tokens, w_qkv, n_tensor * n_req)
    tokens = lax.all_to_all(spread, ("tensor", "req"), split_axis=0, concat_axis=0, tiled=True)
    if n_tensor == 2:
        blocks = (block, swapped(block))
    else:
        blocks = (lax.all_gather(block, "tensor", axis=1, tiled=True),)
    pre_term, dec_row, own = attend(blocks, w_q, w_qkv, w_out)
    tokens, own = lax.optimization_barrier((tokens, own))
    sent = pages(lists, tokens, w_q, cache_keys, cache_values, n_tensor)
    sent, pre_term = lax.optimization_barrier((sent, pre_term))
    axes = ("tensor", "req") if n_tensor == 2 else "req"
    got = lax.all_to_all(sent, axes, split_axis=0, concat_axis=0, tiled=True)
    pre_first, pre_mlp = mlp(blocks, gathered_terms(pre_term), gain1, bias1, w_up, w_down)
    own, pre_mlp = lax.optimization_barrier((own, pre_mlp))
    dec_term = join(got, own, w_out, n_req)
    dec_term, pre_mlp = lax.optimization_barrier((dec_term, pre_mlp))
    pre_groups = gathered_terms(pre_mlp)
    dec_first, hidden = up(dec_row, gathered_terms(dec_term), gain1, bias1, w_up)
    pre_out = finish(pre_first, [group[0] for group in pre_groups], gain2, bias2, pre_len, cols, "pre_norm")
    hidden, pre_out = lax.optimization_barrier((hidden, pre_out))
    dec_mlp = down(hidden, w_down)
    dec_groups = gathered_terms(dec_mlp)
    dec_out = finish(dec_first, [group[0] for group in dec_groups], gain2, bias2, 1, cols, "dec_norm")
    return (pre_out, dec_out)


def solution(mesh):
    in_specs = (
        P("req", "tensor"),
        P("req", "tensor"),
        P(),
        P(),
        P(),
        P(),
        P("req", None, "tensor"),
        P("req", None, "tensor"),
        P(None, None, "tensor"),
        P("tensor", None),
        P(),
        P(),
        P(None, "tensor"),
        P("tensor", None),
        P(),
        P(),
    )
    out_specs = (P("req", "tensor"), P("req", "tensor"))
    return jax.shard_map(local, mesh=mesh, in_specs=in_specs, out_specs=out_specs, check_vma=False)
```

```python
import functools
import math

import jax
import jax.numpy as jnp
from jax import lax
from jax.experimental import pallas as pl
from jax.experimental.pallas import tpu as pltpu
from jax.sharding import PartitionSpec as P

HD = 64
LANES = 128
TAIL = 16
NORM_EPS = 1e-05
NEG_LARGE = -1e30
BF16 = jnp.bfloat16
F32 = jnp.float32

VMEM = pl.BlockSpec(memory_space=pltpu.VMEM)
HBM = pl.BlockSpec(memory_space=pltpu.HBM)


def in_hbm(x):
    return pltpu.with_memory_space_constraint(x, pltpu.HBM)


def like(x):
    return jax.ShapeDtypeStruct(x.shape, x.dtype)


def params(mib):
    return pltpu.CompilerParams(vmem_limit_bytes=mib << 20)


def cost(flops=1):
    return pl.CostEstimate(flops=flops, bytes_accessed=1, transcendentals=0)


def start_all(copies):
    @pl.loop(0, jnp.where(lax.axis_index("req") >= 0, 1, 0))
    def _(_):
        for copy in copies:
            copy.start()


def dot(left, right):
    return jnp.dot(left, right, preferred_element_type=F32)


def dot_t(left, right):
    return lax.dot_general(left, right, (((1,), (1,)), ((), ())), preferred_element_type=F32)


def norm_rows(total, gain, shift):
    mean = jnp.mean(total, axis=-1, keepdims=True)
    centered = total - mean
    var = jnp.mean(centered * centered, axis=-1, keepdims=True)
    return centered * lax.rsqrt(var + NORM_EPS) * gain + shift


def gelu(x):
    return 0.5 * x * (1.0 + lax.erf(x * (1.0 / math.sqrt(2.0))))


def head_mask(rows, cols):
    head = lax.broadcasted_iota(jnp.int32, (rows, cols), 0)
    lane = lax.broadcasted_iota(jnp.int32, (rows, cols), 1)
    return lane // HD == head


def start_kernel(token_hbm, chunk_hbm, w_qkv_hbm, out_hbm, block, w_q, out, token, sems):
    pre_len = chunk_hbm.shape[0]
    fetch = pltpu.make_async_copy(token_hbm, token, sems.at[0])
    rows = pltpu.make_async_copy(chunk_hbm, block.at[pl.ds(0, pre_len)], sems.at[1])
    weights = pltpu.make_async_copy(w_qkv_hbm.at[0], w_q, sems.at[3])
    start_all((fetch, rows, weights))
    fetch.wait()
    own = token[...].astype(F32)
    for r in range(out.shape[1]):
        out[:, r, :] = jnp.broadcast_to(own[:, r * LANES : (r + 1) * LANES], (out.shape[0], LANES))
    spread = pltpu.make_async_copy(out, out_hbm, sems.at[2])
    start_all((spread,))
    is_first = lax.broadcasted_iota(jnp.int32, (TAIL, own.shape[1]), 0) == 0
    block[pre_len:, :] = jnp.where(is_first, own, 0.0).astype(BF16)
    rows.wait()
    spread.wait()
    weights.wait()


def start(token, chunk, w_qkv, count):
    pre_len, cols = chunk.shape
    return pl.pallas_call(
        start_kernel,
        in_specs=[HBM] * 3,
        out_specs=[HBM, VMEM, VMEM],
        out_shape=[
            pltpu.HBM((count, cols // LANES, LANES), F32),
            jax.ShapeDtypeStruct((pre_len + TAIL, cols), BF16),
            jax.ShapeDtypeStruct(w_qkv.shape[1:], BF16),
        ],
        scratch_shapes=[
            pltpu.VMEM((count, cols // LANES, LANES), F32),
            pltpu.VMEM(token.shape, BF16),
            pltpu.SemaphoreType.DMA((4,)),
        ],
        compiler_params=params(8),
        cost_estimate=cost(),
        name="start",
    )(in_hbm(token), in_hbm(chunk), in_hbm(w_qkv))


def row_copies(blocks, count, rows, sems):
    part = lax.axis_index("tensor")
    copies = []
    for c, block in enumerate(blocks):
        wide = block.shape[1]
        offset = part * wide if c == 0 else (1 - part) * wide
        band = pl.ds(pl.multiple_of(offset, LANES), wide) if len(blocks) > 1 else slice(None)
        copies.append(pltpu.make_async_copy(block.at[pl.ds(0, count)], rows.at[:, band], sems.at[c]))
    return copies


def pages_kernel(n_tensor, values_hbm, req_of, table, place, lengths, tokens, w_q, keys, sent, values, sem):
    fetch = pltpu.make_async_copy(values_hbm, values, sem)
    start_all((fetch,))
    n_req, max_pages = table.shape
    cols = w_q.shape[1]
    pieces = cols // LANES
    pages_here, page_len = keys.shape[:2]
    heads = max(8, cols // HD)
    me = lax.axis_index("req")
    part = lax.axis_index("tensor")
    x = jnp.concatenate(
        [tokens[t * n_req : (t + 1) * n_req, r, :] for t in range(n_tensor) for r in range(pieces)],
        axis=1,
    )
    q = dot(x.astype(BF16), w_q[...]).astype(BF16).astype(F32) * (1.0 / math.sqrt(HD))

    slot_row = lax.broadcasted_iota(jnp.int32, (n_req, n_req), 0)
    slot_col = lax.broadcasted_iota(jnp.int32, (n_req, n_req), 1)
    request = jnp.sum(jnp.where(slot_row == slot_col, req_of[...], 0), axis=1, keepdims=True)
    served = request == slot_col
    length = jnp.sum(jnp.where(served, lengths[...], 0), axis=1, keepdims=True)
    ids = jnp.dot(
        served.astype(F32),
        table[...].astype(F32),
        precision=lax.Precision.HIGHEST,
        preferred_element_type=F32,
    ).astype(jnp.int32)
    at_page = lax.broadcasted_iota(jnp.int32, (n_req, max_pages), 1)
    left = length - at_page * page_len
    page_ids = lax.broadcasted_iota(jnp.int32, place.shape, 1)
    owners = []
    usable = []
    for p in range(pages_here):
        page = jnp.sum(jnp.where(place[...] == me * pages_here + p, page_ids, 0), axis=1, keepdims=True)
        hit = ids == page
        owners.append(jnp.sum(jnp.where(hit, 1.0, 0.0), axis=1, keepdims=True))
        count = jnp.sum(jnp.where(hit, left, 0), axis=1, keepdims=True)
        usable.append(jnp.sum(count, axis=0, keepdims=True))

    mask = head_mask(heads, cols)
    token = lax.broadcasted_iota(jnp.int32, (heads, page_len), 1)

    def spread(per_head):
        return jnp.sum(jnp.where(mask, per_head, 0.0), axis=0, keepdims=True)

    scores = []
    for p in range(pages_here):
        query = jnp.sum(owners[p] * q, axis=0, keepdims=True)
        query = jnp.where(mask, query, 0.0).astype(BF16)
        scores.append(jnp.where(token < usable[p], dot_t(query, keys[p]), NEG_LARGE))
    scores = jnp.concatenate(scores, axis=0)
    top = jnp.max(scores, axis=-1, keepdims=True)
    weights = jnp.exp(scores - top)
    total = jnp.sum(weights, axis=-1, keepdims=True)
    level = top + jnp.log(total)
    weights = weights.astype(BF16)
    fetch.wait()
    context = jnp.zeros((n_req, cols), F32)
    levels = (1.0 - sum(owners)) * jnp.full((n_req, cols), NEG_LARGE, F32)
    for p in range(pages_here):
        at = slice(p * heads, (p + 1) * heads)
        context = context + owners[p] * spread(dot(weights[at], values[p]) / total[at])
        levels = levels + owners[p] * spread(level[at])
    to = pl.ds(pl.multiple_of(part * n_req, n_req), n_req) if n_tensor == 2 else slice(None)
    if n_tensor == 2:
        sent[...] = jnp.zeros(sent.shape, F32)
    for r in range(pieces):
        sent[to, r, :] = context[:, r * LANES : (r + 1) * LANES]
        sent[to, pieces + r, :] = levels[:, r * LANES : (r + 1) * LANES]


def pages(lists, tokens, w_q, keys, values, n_tensor):
    cols = w_q.shape[1]
    n_req = lists[0].shape[0]
    twice = 2 * (cols // LANES)
    req_of, table, place, lengths = lists
    return pl.pallas_call(
        functools.partial(pages_kernel, n_tensor),
        in_specs=[HBM] + [VMEM] * 7,
        out_specs=VMEM,
        scratch_shapes=[pltpu.VMEM(values.shape, BF16), pltpu.SemaphoreType.DMA],
        out_shape=jax.ShapeDtypeStruct((n_req * (2 if n_tensor == 2 else 1), twice, LANES), F32),
        compiler_params=params(12),
        cost_estimate=cost(),
        name="pages",
    )(
        in_hbm(values),
        req_of.reshape(1, -1),
        table,
        place.reshape(1, -1),
        lengths.reshape(1, -1),
        tokens,
        w_q,
        keys,
    )


def attend_kernel(n_blocks, w_qkv_hbm, w_out_hbm, w_q, *refs):
    blocks = refs[:n_blocks]
    term, dec_row, own, rows, w_kv, w_out, ctx, sems = refs[n_blocks:]
    count = rows.shape[0]
    pre_len = count - TAIL
    inputs = row_copies(blocks, count, rows, sems)
    sources = (w_qkv_hbm.at[1], w_qkv_hbm.at[2], w_out_hbm)
    targets = (w_kv.at[0], w_kv.at[1], w_out)
    copies = [
        pltpu.make_async_copy(source, target, sems.at[n_blocks + i])
        for i, (source, target) in enumerate(zip(sources, targets))
    ]
    start_all((*inputs, copies[0]))
    for copy in inputs:
        copy.wait()
    dec_row[...] = rows[pre_len:, :]
    cols = w_q.shape[1]
    pieces = cols // LANES
    half = pre_len // 2
    x = rows[...]
    q = dot(x, w_q[...]).astype(BF16) * jnp.asarray(1.0 / math.sqrt(HD), BF16)
    start_all(copies[1:])
    copies[0].wait()
    k = dot(x, w_kv[0]).astype(BF16)

    low = lax.broadcasted_iota(jnp.int32, (half, LANES), 1) < HD
    row = lax.broadcasted_iota(jnp.int32, (2 * half, half), 0)
    col = lax.broadcasted_iota(jnp.int32, (2 * half, half), 1)
    causal = jnp.where(row >= half, row - half, row) >= col
    zero = jnp.zeros((), BF16)
    jobs = []
    for g in range(pieces):
        at = slice(g * LANES, (g + 1) * LANES)
        for block in range(2):
            mine = slice(block * half, (block + 1) * half)
            qg = q[mine, at]
            both = jnp.concatenate([jnp.where(low, qg, zero), jnp.where(low, zero, qg)], axis=0)
            scores = jnp.where(causal, dot_t(both, k[mine, at]), NEG_LARGE)
            if block:
                scores = jnp.concatenate([dot_t(both, k[:half, at]), scores], axis=1)
            jobs.append((mine, at, scores))
    weights = []
    for _, _, scores in jobs:
        top = jnp.max(scores, axis=-1, keepdims=True)
        weights.append(jnp.exp(scores - top).astype(BF16))

    copies[1].wait()
    v = dot(x, w_kv[1]).astype(BF16)
    heads = max(8, cols // HD)
    mask = head_mask(heads, cols)
    own_q, own_k, own_v = (part[pre_len:].astype(F32)[:1] for part in (q, k, v))
    own_score = jnp.sum(jnp.where(mask, own_q * own_k, 0.0), axis=1, keepdims=True)
    own[0:1, :] = own_v
    own[1:2, :] = jnp.sum(jnp.where(mask, own_score, 0.0), axis=0, keepdims=True)

    ones = jnp.ones((pre_len, LANES), BF16)
    for (mine, at, _), weight in zip(jobs, weights):
        values = jnp.concatenate([v[: mine.stop, at], ones[: mine.stop]], axis=1)
        out = dot(weight, values)
        out = out[:, :LANES] / out[:, LANES:]
        ctx[mine, at] = jnp.where(low, out[:half], out[half:]).astype(BF16)

    copies[2].wait()
    term[...] = dot(ctx[...], w_out[...]).astype(BF16)


def attend(blocks, w_q, w_qkv, w_out):
    width, cols = w_qkv.shape[1:]
    count = blocks[0].shape[0]
    return pl.pallas_call(
        functools.partial(attend_kernel, len(blocks)),
        in_specs=[HBM] * 2 + [VMEM] * (1 + len(blocks)),
        out_specs=[VMEM] * 3,
        out_shape=[
            jax.ShapeDtypeStruct((count - TAIL, width), BF16),
            jax.ShapeDtypeStruct((TAIL, width), BF16),
            jax.ShapeDtypeStruct((2, cols), F32),
        ],
        scratch_shapes=[
            pltpu.VMEM((count, width), BF16),
            pltpu.VMEM((2, width, cols), BF16),
            pltpu.VMEM(w_out.shape, BF16),
            pltpu.VMEM((count - TAIL, cols), BF16),
            pltpu.SemaphoreType.DMA((3 + len(blocks),)),
        ],
        compiler_params=params(20),
        cost_estimate=cost(),
        name="attend",
    )(in_hbm(w_qkv), in_hbm(w_out), w_q, *blocks)


def join_kernel(n_req, got, own, w_out, term):
    cols = own.shape[1]
    pieces = cols // LANES
    sources = slice(None)
    if got.shape[0] > n_req:
        sources = pl.ds(pl.multiple_of(lax.axis_index("tensor") * n_req, n_req), n_req)
    context = []
    for g in range(pieces):
        at = slice(g * LANES, (g + 1) * LANES)
        level = got[sources, pieces + g, :]
        own_level = own[1:2, at]
        top = jnp.maximum(jnp.max(level, axis=0, keepdims=True), own_level)
        share = jnp.exp(level - top)
        own_share = jnp.exp(own_level - top)
        numer = jnp.sum(share * got[sources, g, :], axis=0, keepdims=True) + own_share * own[0:1, at]
        context.append(numer / (jnp.sum(share, axis=0, keepdims=True) + own_share))
    context = jnp.broadcast_to(jnp.concatenate(context, axis=1), (TAIL, cols))
    term[...] = dot(context.astype(BF16), w_out[...]).astype(BF16)


def join(got, own, w_out, n_req):
    return pl.pallas_call(
        functools.partial(join_kernel, n_req),
        in_specs=[VMEM] * 3,
        out_specs=VMEM,
        out_shape=jax.ShapeDtypeStruct((TAIL, w_out.shape[1]), BF16),
        compiler_params=params(8),
        cost_estimate=cost(6_000_000_000),
        name="join",
    )(got, own, w_out)


def first_rows(rows, terms, gain, shift):
    attn = 0.0
    for group in terms:
        attn = attn + jnp.concatenate([part[...].astype(F32) for part in group], axis=0)
    return norm_rows(rows.astype(F32) + attn, gain[...], shift[...]).astype(BF16)


def split_refs(refs, counts):
    groups = []
    for count in counts:
        groups.append(refs[:count])
        refs = refs[count:]
    return groups, refs


def mlp_kernel(n_blocks, counts, tile, w_up_hbm, w_down_hbm, *refs):
    blocks = refs[:n_blocks]
    terms, refs = split_refs(refs[n_blocks:], counts)
    gain, shift, first_ref, term, rows, w_up, w_down, sems = refs
    units = w_up.shape[1]
    steps = range(0, units, tile)
    inputs = row_copies(blocks, rows.shape[0], rows, sems)
    ups, downs = [], []
    for i, unit in enumerate(steps):
        part = pl.ds(unit, tile)
        at = n_blocks + 2 * i
        ups.append(pltpu.make_async_copy(w_up_hbm.at[:, part], w_up.at[:, part], sems.at[at]))
        downs.append(pltpu.make_async_copy(w_down_hbm.at[part], w_down.at[part], sems.at[at + 1]))
    start_all((*inputs, *ups, *downs))
    for copy in inputs:
        copy.wait()
    first = first_rows(rows[...], terms, gain, shift)
    first_ref[...] = first
    hidden = []
    for unit, copy in zip(steps, ups):
        copy.wait()
        hidden.append(gelu(dot(first, w_up[:, unit : unit + tile])).astype(BF16))
    total = 0.0
    for i, copy in enumerate(downs):
        copy.wait()
        total = total + dot(hidden[i], w_down[i * tile : (i + 1) * tile, :])
    term[...] = total.astype(BF16)


def mlp(blocks, terms, gain, shift, w_up, w_down):
    counts = [len(group) for group in terms]
    count = blocks[0].shape[0] - TAIL
    width, units = w_up.shape
    tile = min(512, units)
    return pl.pallas_call(
        functools.partial(mlp_kernel, len(blocks), counts, tile),
        in_specs=[HBM] * 2 + [VMEM] * (2 + len(blocks) + sum(counts)),
        out_specs=[VMEM] * 2,
        out_shape=[jax.ShapeDtypeStruct((count, width), BF16)] * 2,
        scratch_shapes=[
            pltpu.VMEM((count, width), BF16),
            pltpu.VMEM(w_up.shape, BF16),
            pltpu.VMEM(w_down.shape, BF16),
            pltpu.SemaphoreType.DMA((len(blocks) + 2 * (units // tile),)),
        ],
        compiler_params=params(28),
        cost_estimate=cost(),
        name="pre_mlp",
    )(in_hbm(w_up), in_hbm(w_down), *blocks, *(part for group in terms for part in group), gain, shift)


def dec_kernel(counts, tile, w_down_hbm, rows, *refs):
    terms, refs = split_refs(refs, counts)
    gain, shift, w_up, first_ref, term, w_down, sems = refs
    copies = []
    for i, unit in enumerate(range(0, w_up.shape[1], tile)):
        part = pl.ds(unit, tile)
        copies.append(pltpu.make_async_copy(w_down_hbm.at[part], w_down.at[part], sems.at[i]))
    start_all(copies)
    first = first_rows(rows[...], terms, gain, shift)
    first_ref[...] = first
    hidden = gelu(dot(first, w_up[...])).astype(BF16)
    total = 0.0
    for i, copy in enumerate(copies):
        part = slice(i * tile, (i + 1) * tile)
        copy.wait()
        total = total + dot(hidden[:, part], w_down[part, :])
    term[...] = total.astype(BF16)


def dec_rows(rows, terms, gain, shift, w_up, w_down):
    counts = [len(group) for group in terms]
    width, units = w_up.shape
    tile = min(512, units)
    return pl.pallas_call(
        functools.partial(dec_kernel, counts, tile),
        in_specs=[HBM] + [VMEM] * (4 + sum(counts)),
        out_specs=[VMEM] * 2,
        out_shape=[jax.ShapeDtypeStruct((TAIL, width), BF16)] * 2,
        scratch_shapes=[pltpu.VMEM(w_down.shape, BF16), pltpu.SemaphoreType.DMA((units // tile,))],
        compiler_params=params(20),
        cost_estimate=cost(),
        name="dec_mlp",
    )(in_hbm(w_down), rows, *(part for group in terms for part in group), gain, shift, w_up)


def finish_kernel(n_terms, first, *refs):
    terms = refs[:n_terms]
    gain, shift, out, scr = refs[n_terms:]
    mlp_sum = terms[0][...].astype(F32)
    for other in terms[1:]:
        mlp_sum = mlp_sum + other[...].astype(F32)
    total = first[...].astype(F32) + mlp_sum
    centered = total - jnp.mean(total, axis=-1, keepdims=True)
    scr[...] = centered
    var = jnp.mean(centered * centered, axis=-1, keepdims=True)
    kept, cols = out.shape
    at = pl.ds(pl.multiple_of(lax.axis_index("tensor") * cols, LANES), cols)
    normed = scr[:, at] * lax.rsqrt(var + NORM_EPS) * gain[:, at] + shift[:, at]
    out[...] = normed[:kept].astype(BF16)


def finish(first, terms, gain, shift, kept, cols, name):
    return pl.pallas_call(
        functools.partial(finish_kernel, len(terms)),
        in_specs=[VMEM] * (3 + len(terms)),
        out_specs=VMEM,
        out_shape=jax.ShapeDtypeStruct((kept, cols), BF16),
        scratch_shapes=[pltpu.VMEM(first.shape, F32)],
        compiler_params=params(12),
        cost_estimate=cost(),
        name=name,
    )(first, *terms, gain, shift)


def local(
    pre_tokens,
    dec_tokens,
    req_of,
    page_table,
    page_place,
    cache_lengths,
    cache_keys,
    cache_values,
    w_qkv,
    w_out,
    ln1_gain,
    ln1_bias,
    w_up,
    w_down,
    ln2_gain,
    ln2_bias,
):
    cols = w_qkv.shape[2]
    n_req = lax.axis_size("req")
    n_tensor = lax.axis_size("tensor")
    w_qkv = jnp.transpose(w_qkv, (1, 0, 2))
    gain1, bias1, gain2, bias2 = (
        jnp.reshape(v, (1, -1)) for v in (ln1_gain, ln1_bias, ln2_gain, ln2_bias)
    )

    def swapped(x):
        return lax.ppermute(x, "tensor", [(0, 1), (1, 0)])

    def gathered_terms(x, cuts=1):
        if n_tensor == 2:
            step = x.shape[0] // cuts
            return ((x,), tuple(swapped(x[i * step : (i + 1) * step]) for i in range(cuts)))
        return ((lax.psum(x, "tensor"),),)

    pre_len = pre_tokens.shape[0]
    lists = (req_of, page_table, page_place, cache_lengths)
    spread, block, w_q = start(dec_tokens, pre_tokens, w_qkv, n_tensor * n_req)
    tokens = lax.all_to_all(spread, ("tensor", "req"), split_axis=0, concat_axis=0, tiled=True)
    if n_tensor == 2:
        blocks = (block, swapped(block))
    else:
        blocks = (lax.all_gather(block, "tensor", axis=1, tiled=True),)
    pre_term, dec_row, own = attend(blocks, w_q, w_qkv, w_out)
    tokens, own = lax.optimization_barrier((tokens, own))
    sent = pages(lists, tokens, w_q, cache_keys, cache_values, n_tensor)
    sent, pre_term = lax.optimization_barrier((sent, pre_term))
    axes = ("tensor", "req") if n_tensor == 2 else "req"
    got = lax.all_to_all(sent, axes, split_axis=0, concat_axis=0, tiled=True)
    pre_first, pre_mlp = mlp(blocks, gathered_terms(pre_term), gain1, bias1, w_up, w_down)
    own, pre_mlp = lax.optimization_barrier((own, pre_mlp))
    dec_groups = gathered_terms(join(got, own, w_out, n_req))
    dec_groups, pre_mlp = lax.optimization_barrier((dec_groups, pre_mlp))
    pre_groups = gathered_terms(pre_mlp)
    dec_first, dec_mlp = dec_rows(dec_row, dec_groups, gain1, bias1, w_up, w_down)
    pre_out = finish(pre_first, [group[0] for group in pre_groups], gain2, bias2, pre_len, cols, "pre_norm")
    dec_first, pre_out = lax.optimization_barrier((dec_first, pre_out))
    dec_groups = gathered_terms(dec_mlp)
    dec_out = finish(dec_first, [group[0] for group in dec_groups], gain2, bias2, 1, cols, "dec_norm")
    return (pre_out, dec_out)


def solution(mesh):
    in_specs = (
        P("req", "tensor"),
        P("req", "tensor"),
        P(),
        P(),
        P(),
        P(),
        P("req", None, "tensor"),
        P("req", None, "tensor"),
        P(None, None, "tensor"),
        P("tensor", None),
        P(),
        P(),
        P(None, "tensor"),
        P("tensor", None),
        P(),
        P(),
    )
    out_specs = (P("req", "tensor"), P("req", "tensor"))
    return jax.shard_map(local, mesh=mesh, in_specs=in_specs, out_specs=out_specs, check_vma=False)
```

```python
import functools
import math

import jax
import jax.numpy as jnp
from jax import lax
from jax.experimental import pallas as pl
from jax.experimental.pallas import tpu as pltpu
from jax.sharding import PartitionSpec as P

HD = 64
LANES = 128
TAIL = 16
NORM_EPS = 1e-05
NEG_LARGE = -1e30
BF16 = jnp.bfloat16
F32 = jnp.float32

VMEM = pl.BlockSpec(memory_space=pltpu.VMEM)
HBM = pl.BlockSpec(memory_space=pltpu.HBM)


def in_hbm(x):
    return pltpu.with_memory_space_constraint(x, pltpu.HBM)


def like(x):
    return jax.ShapeDtypeStruct(x.shape, x.dtype)


def params(mib):
    return pltpu.CompilerParams(vmem_limit_bytes=mib << 20)


def cost(flops=1):
    return pl.CostEstimate(flops=flops, bytes_accessed=1, transcendentals=0)


def start_all(copies):
    @pl.loop(0, jnp.where(lax.axis_index("req") >= 0, 1, 0))
    def _(_):
        for copy in copies:
            copy.start()


def dot(left, right):
    return jnp.dot(left, right, preferred_element_type=F32)


def dot_t(left, right):
    return lax.dot_general(left, right, (((1,), (1,)), ((), ())), preferred_element_type=F32)


def norm_rows(total, gain, shift):
    mean = jnp.mean(total, axis=-1, keepdims=True)
    centered = total - mean
    var = jnp.mean(centered * centered, axis=-1, keepdims=True)
    return centered * lax.rsqrt(var + NORM_EPS) * gain + shift


def gelu(x):
    return 0.5 * x * (1.0 + lax.erf(x * (1.0 / math.sqrt(2.0))))


def head_mask(rows, cols):
    head = lax.broadcasted_iota(jnp.int32, (rows, cols), 0)
    lane = lax.broadcasted_iota(jnp.int32, (rows, cols), 1)
    return lane // HD == head


def start_kernel(token_hbm, chunk_hbm, w_qkv_hbm, out_hbm, block, w_q, out, token, sems):
    pre_len = chunk_hbm.shape[0]
    fetch = pltpu.make_async_copy(token_hbm, token, sems.at[0])
    rows = pltpu.make_async_copy(chunk_hbm, block.at[pl.ds(0, pre_len)], sems.at[1])
    weights = pltpu.make_async_copy(w_qkv_hbm.at[0], w_q, sems.at[3])
    start_all((fetch, rows, weights))
    fetch.wait()
    own = token[...].astype(F32)
    for r in range(out.shape[1]):
        out[:, r, :] = jnp.broadcast_to(own[:, r * LANES : (r + 1) * LANES], (out.shape[0], LANES))
    spread = pltpu.make_async_copy(out, out_hbm, sems.at[2])
    start_all((spread,))
    is_first = lax.broadcasted_iota(jnp.int32, (TAIL, own.shape[1]), 0) == 0
    block[pre_len:, :] = jnp.where(is_first, own, 0.0).astype(BF16)
    rows.wait()
    spread.wait()
    weights.wait()


def start(token, chunk, w_qkv, count):
    pre_len, cols = chunk.shape
    return pl.pallas_call(
        start_kernel,
        in_specs=[HBM] * 3,
        out_specs=[HBM, VMEM, VMEM],
        out_shape=[
            pltpu.HBM((count, cols // LANES, LANES), F32),
            jax.ShapeDtypeStruct((pre_len + TAIL, cols), BF16),
            jax.ShapeDtypeStruct(w_qkv.shape[1:], BF16),
        ],
        scratch_shapes=[
            pltpu.VMEM((count, cols // LANES, LANES), F32),
            pltpu.VMEM(token.shape, BF16),
            pltpu.SemaphoreType.DMA((4,)),
        ],
        compiler_params=params(8),
        cost_estimate=cost(),
        name="start",
    )(in_hbm(token), in_hbm(chunk), in_hbm(w_qkv))


def row_copies(blocks, count, rows, sems):
    part = lax.axis_index("tensor")
    copies = []
    for c, block in enumerate(blocks):
        wide = block.shape[1]
        offset = part * wide if c == 0 else (1 - part) * wide
        band = pl.ds(pl.multiple_of(offset, LANES), wide) if len(blocks) > 1 else slice(None)
        copies.append(pltpu.make_async_copy(block.at[pl.ds(0, count)], rows.at[:, band], sems.at[c]))
    return copies


def pages_kernel(n_tensor, values_hbm, req_of, table, place, lengths, tokens, w_q, keys, sent, values, sems):
    half = values.shape[0] // 2 + 1
    parts = [pl.ds(0, half), pl.ds(half, values.shape[0] - half)]
    fetches = [
        pltpu.make_async_copy(values_hbm.at[part], values.at[part], sems.at[i]) for i, part in enumerate(parts)
    ]
    start_all(fetches)
    n_req, max_pages = table.shape
    cols = w_q.shape[1]
    pieces = cols // LANES
    pages_here, page_len = keys.shape[:2]
    heads = max(8, cols // HD)
    me = lax.axis_index("req")
    part = lax.axis_index("tensor")
    x = jnp.concatenate(
        [tokens[t * n_req : (t + 1) * n_req, r, :] for t in range(n_tensor) for r in range(pieces)],
        axis=1,
    )
    q = dot(x.astype(BF16), w_q[...]).astype(BF16).astype(F32) * (1.0 / math.sqrt(HD))

    slot_row = lax.broadcasted_iota(jnp.int32, (n_req, n_req), 0)
    slot_col = lax.broadcasted_iota(jnp.int32, (n_req, n_req), 1)
    request = jnp.sum(jnp.where(slot_row == slot_col, req_of[...], 0), axis=1, keepdims=True)
    served = request == slot_col
    length = jnp.sum(jnp.where(served, lengths[...], 0), axis=1, keepdims=True)
    ids = jnp.dot(
        served.astype(F32),
        table[...].astype(F32),
        precision=lax.Precision.HIGHEST,
        preferred_element_type=F32,
    ).astype(jnp.int32)
    at_page = lax.broadcasted_iota(jnp.int32, (n_req, max_pages), 1)
    left = length - at_page * page_len
    page_ids = lax.broadcasted_iota(jnp.int32, place.shape, 1)
    owners = []
    usable = []
    for p in range(pages_here):
        page = jnp.sum(jnp.where(place[...] == me * pages_here + p, page_ids, 0), axis=1, keepdims=True)
        hit = ids == page
        owners.append(jnp.sum(jnp.where(hit, 1.0, 0.0), axis=1, keepdims=True))
        count = jnp.sum(jnp.where(hit, left, 0), axis=1, keepdims=True)
        usable.append(jnp.sum(count, axis=0, keepdims=True))

    mask = head_mask(heads, cols)
    token = lax.broadcasted_iota(jnp.int32, (heads, page_len), 1)

    def spread(per_head):
        return jnp.sum(jnp.where(mask, per_head, 0.0), axis=0, keepdims=True)

    scores = []
    for p in range(pages_here):
        query = jnp.sum(owners[p] * q, axis=0, keepdims=True)
        query = jnp.where(mask, query, 0.0).astype(BF16)
        scores.append(jnp.where(token < usable[p], dot_t(query, keys[p]), NEG_LARGE))
    scores = jnp.concatenate(scores, axis=0)
    top = jnp.max(scores, axis=-1, keepdims=True)
    weights = jnp.exp(scores - top)
    total = jnp.sum(weights, axis=-1, keepdims=True)
    level = top + jnp.log(total)
    weights = weights.astype(BF16)
    context = jnp.zeros((n_req, cols), F32)
    levels = (1.0 - sum(owners)) * jnp.full((n_req, cols), NEG_LARGE, F32)
    for p in range(pages_here):
        if p in (0, half):
            fetches[p // half].wait()
        at = slice(p * heads, (p + 1) * heads)
        context = context + owners[p] * spread(dot(weights[at], values[p]) / total[at])
        levels = levels + owners[p] * spread(level[at])
    to = pl.ds(pl.multiple_of(part * n_req, n_req), n_req) if n_tensor == 2 else slice(None)
    if n_tensor == 2:
        sent[...] = jnp.zeros(sent.shape, F32)
    for r in range(pieces):
        sent[to, r, :] = context[:, r * LANES : (r + 1) * LANES]
        sent[to, pieces + r, :] = levels[:, r * LANES : (r + 1) * LANES]


def pages(lists, tokens, w_q, keys, values, n_tensor):
    cols = w_q.shape[1]
    n_req = lists[0].shape[0]
    twice = 2 * (cols // LANES)
    req_of, table, place, lengths = lists
    return pl.pallas_call(
        functools.partial(pages_kernel, n_tensor),
        in_specs=[HBM] + [VMEM] * 7,
        out_specs=VMEM,
        scratch_shapes=[pltpu.VMEM(values.shape, BF16), pltpu.SemaphoreType.DMA((2,))],
        out_shape=jax.ShapeDtypeStruct((n_req * (2 if n_tensor == 2 else 1), twice, LANES), F32),
        compiler_params=params(12),
        cost_estimate=cost(),
        name="pages",
    )(
        in_hbm(values),
        req_of.reshape(1, -1),
        table,
        place.reshape(1, -1),
        lengths.reshape(1, -1),
        tokens,
        w_q,
        keys,
    )


def attend_kernel(n_blocks, w_qkv_hbm, w_out_hbm, w_q, *refs):
    blocks = refs[:n_blocks]
    term, dec_row, own, rows, w_kv, w_out, ctx, sems = refs[n_blocks:]
    count = rows.shape[0]
    pre_len = count - TAIL
    inputs = row_copies(blocks, count, rows, sems)
    sources = (w_qkv_hbm.at[1], w_qkv_hbm.at[2], w_out_hbm)
    targets = (w_kv.at[0], w_kv.at[1], w_out)
    copies = [
        pltpu.make_async_copy(source, target, sems.at[n_blocks + i])
        for i, (source, target) in enumerate(zip(sources, targets))
    ]
    start_all((*inputs, copies[0]))
    for copy in inputs:
        copy.wait()
    dec_row[...] = rows[pre_len:, :]
    cols = w_q.shape[1]
    pieces = cols // LANES
    half = pre_len // 2
    x = rows[...]
    q = dot(x, w_q[...]).astype(BF16) * jnp.asarray(1.0 / math.sqrt(HD), BF16)
    start_all(copies[1:])
    copies[0].wait()
    k = dot(x, w_kv[0]).astype(BF16)

    low = lax.broadcasted_iota(jnp.int32, (half, LANES), 1) < HD
    row = lax.broadcasted_iota(jnp.int32, (2 * half, half), 0)
    col = lax.broadcasted_iota(jnp.int32, (2 * half, half), 1)
    causal = jnp.where(row >= half, row - half, row) >= col
    zero = jnp.zeros((), BF16)
    jobs = []
    for g in range(pieces):
        at = slice(g * LANES, (g + 1) * LANES)
        for block in range(2):
            mine = slice(block * half, (block + 1) * half)
            qg = q[mine, at]
            both = jnp.concatenate([jnp.where(low, qg, zero), jnp.where(low, zero, qg)], axis=0)
            scores = jnp.where(causal, dot_t(both, k[mine, at]), NEG_LARGE)
            if block:
                scores = jnp.concatenate([dot_t(both, k[:half, at]), scores], axis=1)
            jobs.append((mine, at, scores))
    weights = []
    for _, _, scores in jobs:
        top = jnp.max(scores, axis=-1, keepdims=True)
        weights.append(jnp.exp(scores - top).astype(BF16))

    copies[1].wait()
    v = dot(x, w_kv[1]).astype(BF16)
    heads = max(8, cols // HD)
    mask = head_mask(heads, cols)
    own_q, own_k, own_v = (part[pre_len:].astype(F32)[:1] for part in (q, k, v))
    own_score = jnp.sum(jnp.where(mask, own_q * own_k, 0.0), axis=1, keepdims=True)
    own[0:1, :] = own_v
    own[1:2, :] = jnp.sum(jnp.where(mask, own_score, 0.0), axis=0, keepdims=True)

    ones = jnp.ones((pre_len, LANES), BF16)
    for (mine, at, _), weight in zip(jobs, weights):
        values = jnp.concatenate([v[: mine.stop, at], ones[: mine.stop]], axis=1)
        out = dot(weight, values)
        out = out[:, :LANES] / out[:, LANES:]
        ctx[mine, at] = jnp.where(low, out[:half], out[half:]).astype(BF16)

    copies[2].wait()
    term[...] = dot(ctx[...], w_out[...]).astype(BF16)


def attend(blocks, w_q, w_qkv, w_out):
    width, cols = w_qkv.shape[1:]
    count = blocks[0].shape[0]
    return pl.pallas_call(
        functools.partial(attend_kernel, len(blocks)),
        in_specs=[HBM] * 2 + [VMEM] * (1 + len(blocks)),
        out_specs=[VMEM] * 3,
        out_shape=[
            jax.ShapeDtypeStruct((count - TAIL, width), BF16),
            jax.ShapeDtypeStruct((TAIL, width), BF16),
            jax.ShapeDtypeStruct((2, cols), F32),
        ],
        scratch_shapes=[
            pltpu.VMEM((count, width), BF16),
            pltpu.VMEM((2, width, cols), BF16),
            pltpu.VMEM(w_out.shape, BF16),
            pltpu.VMEM((count - TAIL, cols), BF16),
            pltpu.SemaphoreType.DMA((3 + len(blocks),)),
        ],
        compiler_params=params(20),
        cost_estimate=cost(),
        name="attend",
    )(in_hbm(w_qkv), in_hbm(w_out), w_q, *blocks)


def join_kernel(n_req, got, own, w_out, term):
    cols = own.shape[1]
    pieces = cols // LANES
    sources = slice(None)
    if got.shape[0] > n_req:
        sources = pl.ds(pl.multiple_of(lax.axis_index("tensor") * n_req, n_req), n_req)
    context = []
    for g in range(pieces):
        at = slice(g * LANES, (g + 1) * LANES)
        level = got[sources, pieces + g, :]
        own_level = own[1:2, at]
        top = jnp.maximum(jnp.max(level, axis=0, keepdims=True), own_level)
        share = jnp.exp(level - top)
        own_share = jnp.exp(own_level - top)
        numer = jnp.sum(share * got[sources, g, :], axis=0, keepdims=True) + own_share * own[0:1, at]
        context.append(numer / (jnp.sum(share, axis=0, keepdims=True) + own_share))
    context = jnp.concatenate(context, axis=1).astype(BF16)
    term[...] = dot(context, w_out[...]).astype(BF16).astype(F32)


def join(got, own, w_out, n_req):
    return pl.pallas_call(
        functools.partial(join_kernel, n_req),
        in_specs=[VMEM] * 3,
        out_specs=VMEM,
        out_shape=jax.ShapeDtypeStruct((1, w_out.shape[1]), F32),
        compiler_params=params(8),
        cost_estimate=cost(6_000_000_000),
        name="join",
    )(got, own, w_out)


def first_rows(rows, terms, gain, shift):
    attn = 0.0
    for group in terms:
        attn = attn + jnp.concatenate([part[...].astype(F32) for part in group], axis=0)
    return norm_rows(rows.astype(F32) + attn, gain[...], shift[...]).astype(BF16)


def split_refs(refs, counts):
    groups = []
    for count in counts:
        groups.append(refs[:count])
        refs = refs[count:]
    return groups, refs


def mlp_kernel(n_blocks, counts, tile, w_up_hbm, w_down_hbm, *refs):
    blocks = refs[:n_blocks]
    terms, refs = split_refs(refs[n_blocks:], counts)
    gain, shift, first_ref, term, rows, w_up, w_down, sems = refs
    units = w_up.shape[1]
    steps = range(0, units, tile)
    inputs = row_copies(blocks, rows.shape[0], rows, sems)
    ups, downs = [], []
    for i, unit in enumerate(steps):
        part = pl.ds(unit, tile)
        at = n_blocks + 2 * i
        ups.append(pltpu.make_async_copy(w_up_hbm.at[:, part], w_up.at[:, part], sems.at[at]))
        downs.append(pltpu.make_async_copy(w_down_hbm.at[part], w_down.at[part], sems.at[at + 1]))
    start_all((*inputs, *ups, *downs))
    for copy in inputs:
        copy.wait()
    first = first_rows(rows[...], terms, gain, shift)
    first_ref[...] = first
    hidden = []
    for unit, copy in zip(steps, ups):
        copy.wait()
        hidden.append(gelu(dot(first, w_up[:, unit : unit + tile])).astype(BF16))
    total = 0.0
    for i, copy in enumerate(downs):
        copy.wait()
        total = total + dot(hidden[i], w_down[i * tile : (i + 1) * tile, :])
    term[...] = total.astype(BF16)


def mlp(blocks, terms, gain, shift, w_up, w_down):
    counts = [len(group) for group in terms]
    count = blocks[0].shape[0] - TAIL
    width, units = w_up.shape
    tile = min(512, units)
    return pl.pallas_call(
        functools.partial(mlp_kernel, len(blocks), counts, tile),
        in_specs=[HBM] * 2 + [VMEM] * (2 + len(blocks) + sum(counts)),
        out_specs=[VMEM] * 2,
        out_shape=[jax.ShapeDtypeStruct((count, width), BF16)] * 2,
        scratch_shapes=[
            pltpu.VMEM((count, width), BF16),
            pltpu.VMEM(w_up.shape, BF16),
            pltpu.VMEM(w_down.shape, BF16),
            pltpu.SemaphoreType.DMA((len(blocks) + 2 * (units // tile),)),
        ],
        compiler_params=params(28),
        cost_estimate=cost(),
        name="pre_mlp",
    )(in_hbm(w_up), in_hbm(w_down), *blocks, *(part for group in terms for part in group), gain, shift)


def dec_kernel(counts, tile, w_down_hbm, rows, *refs):
    terms, refs = split_refs(refs, counts)
    gain, shift, w_up, first_ref, term, w_down, sems = refs
    copies = []
    for i, unit in enumerate(range(0, w_up.shape[1], tile)):
        part = pl.ds(unit, tile)
        copies.append(pltpu.make_async_copy(w_down_hbm.at[part], w_down.at[part], sems.at[i]))
    start_all(copies)
    first = first_rows(rows[...], terms, gain, shift)
    first_ref[...] = first
    hidden = gelu(dot(first, w_up[...])).astype(BF16)
    total = 0.0
    for i, copy in enumerate(copies):
        part = slice(i * tile, (i + 1) * tile)
        copy.wait()
        total = total + dot(hidden[:, part], w_down[part, :])
    term[...] = total[:1].astype(BF16).astype(F32)


def dec_rows(rows, terms, gain, shift, w_up, w_down):
    counts = [len(group) for group in terms]
    width, units = w_up.shape
    tile = min(512, units)
    return pl.pallas_call(
        functools.partial(dec_kernel, counts, tile),
        in_specs=[HBM] + [VMEM] * (4 + sum(counts)),
        out_specs=[VMEM] * 2,
        out_shape=[jax.ShapeDtypeStruct((TAIL, width), BF16), jax.ShapeDtypeStruct((1, width), F32)],
        scratch_shapes=[pltpu.VMEM(w_down.shape, BF16), pltpu.SemaphoreType.DMA((units // tile,))],
        compiler_params=params(20),
        cost_estimate=cost(),
        name="dec_mlp",
    )(in_hbm(w_down), rows, *(part for group in terms for part in group), gain, shift, w_up)


def finish_kernel(n_terms, first, *refs):
    terms = refs[:n_terms]
    gain, shift, out, scr = refs[n_terms:]
    mlp_sum = terms[0][...].astype(F32)
    for other in terms[1:]:
        mlp_sum = mlp_sum + other[...].astype(F32)
    total = first[...].astype(F32) + mlp_sum
    centered = total - jnp.mean(total, axis=-1, keepdims=True)
    scr[...] = centered
    var = jnp.mean(centered * centered, axis=-1, keepdims=True)
    kept, cols = out.shape
    at = pl.ds(pl.multiple_of(lax.axis_index("tensor") * cols, LANES), cols)
    normed = scr[:, at] * lax.rsqrt(var + NORM_EPS) * gain[:, at] + shift[:, at]
    out[...] = normed[:kept].astype(BF16)


def finish(first, terms, gain, shift, kept, cols, name):
    return pl.pallas_call(
        functools.partial(finish_kernel, len(terms)),
        in_specs=[VMEM] * (3 + len(terms)),
        out_specs=VMEM,
        out_shape=jax.ShapeDtypeStruct((kept, cols), BF16),
        scratch_shapes=[pltpu.VMEM(first.shape, F32)],
        compiler_params=params(12),
        cost_estimate=cost(),
        name=name,
    )(first, *terms, gain, shift)


def local(
    pre_tokens,
    dec_tokens,
    req_of,
    page_table,
    page_place,
    cache_lengths,
    cache_keys,
    cache_values,
    w_qkv,
    w_out,
    ln1_gain,
    ln1_bias,
    w_up,
    w_down,
    ln2_gain,
    ln2_bias,
):
    cols = w_qkv.shape[2]
    n_req = lax.axis_size("req")
    n_tensor = lax.axis_size("tensor")
    w_qkv = jnp.transpose(w_qkv, (1, 0, 2))
    gain1, bias1, gain2, bias2 = (
        jnp.reshape(v, (1, -1)) for v in (ln1_gain, ln1_bias, ln2_gain, ln2_bias)
    )

    def swapped(x):
        return lax.ppermute(x, "tensor", [(0, 1), (1, 0)])

    def gathered_terms(x, cuts=1):
        if n_tensor == 2:
            step = x.shape[0] // cuts
            return ((x,), tuple(swapped(x[i * step : (i + 1) * step]) for i in range(cuts)))
        return ((lax.psum(x, "tensor"),),)

    pre_len = pre_tokens.shape[0]
    lists = (req_of, page_table, page_place, cache_lengths)
    spread, block, w_q = start(dec_tokens, pre_tokens, w_qkv, n_tensor * n_req)
    tokens = lax.all_to_all(spread, ("tensor", "req"), split_axis=0, concat_axis=0, tiled=True)
    if n_tensor == 2:
        blocks = (block, swapped(block))
    else:
        blocks = (lax.all_gather(block, "tensor", axis=1, tiled=True),)
    pre_term, dec_row, own = attend(blocks, w_q, w_qkv, w_out)
    tokens, own = lax.optimization_barrier((tokens, own))
    sent = pages(lists, tokens, w_q, cache_keys, cache_values, n_tensor)
    sent, pre_term = lax.optimization_barrier((sent, pre_term))
    axes = ("tensor", "req") if n_tensor == 2 else "req"
    got = lax.all_to_all(sent, axes, split_axis=0, concat_axis=0, tiled=True)
    pre_first, pre_mlp = mlp(blocks, gathered_terms(pre_term), gain1, bias1, w_up, w_down)
    own, pre_mlp = lax.optimization_barrier((own, pre_mlp))
    dec_groups = gathered_terms(join(got, own, w_out, n_req))
    dec_groups, pre_mlp = lax.optimization_barrier((dec_groups, pre_mlp))
    pre_groups = gathered_terms(pre_mlp)
    dec_first, dec_mlp = dec_rows(dec_row, dec_groups, gain1, bias1, w_up, w_down)
    pre_out = finish(pre_first, [group[0] for group in pre_groups], gain2, bias2, pre_len, cols, "pre_norm")
    dec_first, pre_out = lax.optimization_barrier((dec_first, pre_out))
    dec_groups = gathered_terms(dec_mlp)
    dec_out = finish(dec_first, [group[0] for group in dec_groups], gain2, bias2, 1, cols, "dec_norm")
    return (pre_out, dec_out)


def solution(mesh):
    in_specs = (
        P("req", "tensor"),
        P("req", "tensor"),
        P(),
        P(),
        P(),
        P(),
        P("req", None, "tensor"),
        P("req", None, "tensor"),
        P(None, None, "tensor"),
        P("tensor", None),
        P(),
        P(),
        P(None, "tensor"),
        P("tensor", None),
        P(),
        P(),
    )
    out_specs = (P("req", "tensor"), P("req", "tensor"))
    return jax.shard_map(local, mesh=mesh, in_specs=in_specs, out_specs=out_specs, check_vma=False)
```
